512 devices in a mesh: ctx: 32 (over y, x, core), dp: 16 (over z).
Axes of the slice: x: 4, y: 4, z: 16, core: 2. Of those that a mesh axis runs over, the one named last changes fastest.
Arguments:
- inputs: bfloat16 [16, 4096, 4096], P('dp', 'ctx'), may hold values from -40 to 40
- grad_output: bfloat16 [16, 4096, 4096], P('dp', 'ctx'), may hold values from -6 to 6
- query_weight: bfloat16 [4096, 512], P('ctx'), may hold values from -1 to 1
- key_weight: bfloat16 [4096, 128], P('ctx'), may hold values from -1 to 1
- value_weight: bfloat16 [4096, 128], P('ctx'), may hold values from -0.09375 to 0.09375
- out_weight: bfloat16 [512, 4096], P(None, 'ctx'), may hold values from -0.25 to 0.25
- doc_lengths: int32 [16, 8], P('dp'), may hold values from 1 to 1024, 4096 in all within a row
- block_order: int32 [16, 64], P('dp'), may hold values from 0 to 63, each once within a row
Outputs:
- grad_input: bfloat16 [16, 4096, 4096], P('dp', 'ctx')
- grad_value_weight: float32 [4096, 128], P('ctx')
The draws below stay inside these ranges and needn't reach their ends.
Inputs may be any that keep to these rules, and one draw needn't show every extreme that they name: `doc_lengths`: each row holds the lengths of the 8 documents of one sequence in order, summing to 4096. `block_order`: each row is a permutation of the 64 blocks of 64 positions.
All inputs are finite; a program needn't handle non-finite values.
Results may differ from the reference program's by a relative error of at most 0.029.
Values may be sent and summed in bfloat16 or wider, within the bound.
No kernel may reach another device: no remote copies, remote signals or barrier semaphores. Data moves between devices by JAX's collectives and lax.ppermute only.
A program may use at most 64 MiB of HBM per device.

```python
import math
import jax
import jax.numpy as jnp
import numpy as np
from jax import lax

D = 4096
HEADS = 4
HD = 128
TOK_DEV = 128
NDOC = 8
SEQ = 4096
NBLK = 64
MAXDOC = 1024
BATCH = 16
N_CTX = 32


def shared_columns(key):
    return jax.random.normal(key, (D, HD), jnp.float32) * D ** (-0.5)


def draw_key_weight(key, part):
    columns = shared_columns(key)
    return jnp.clip(columns, -1.0, 1.0).astype(jnp.bfloat16)


def draw_query_weight(key, part):
    key = jax.random.fold_in(key, 12)
    own_part = jax.random.normal(key, (D, HEADS * HD), jnp.float32) * D ** (-0.5)
    return jnp.clip(own_part, -1.0, 1.0).astype(jnp.bfloat16)


def draw_inputs(key, part):
    key = jax.random.fold_in(key, 13)
    first_key = jax.random.fold_in(key, 0)
    shape = (BATCH, SEQ, D)
    values = jax.random.normal(first_key, shape, jnp.float32)
    return jnp.clip(values, -40.0, 40.0).astype(jnp.bfloat16)


def block_levels(key, extent, cuts, low, largest):
    loudness, own = 1.0, jax.random.fold_in(key, 6)
    for dim, parts in cuts:
        heights = jnp.exp(jax.random.uniform(jax.random.fold_in(own, dim), (parts,), jnp.float32, low / len(cuts), largest / len(cuts)))
        loudness = loudness * jnp.repeat(heights, extent[dim] // parts).reshape([-1 if axis == dim else 1 for axis in range(len(extent))])
    return loudness


def profile(amount, total, most, lean):
    portions = [(1 << 20) // math.isqrt(rank ** lean) + 1 for rank in range(2, amount + 1)]
    spare, counts = total - most - (amount - 1), [1] * (amount - 1)
    while spare > 0:
        candidates = [i for i in range(amount - 1) if counts[i] < most]
        mass, remaining = sum([portions[i] for i in candidates]), spare
        for i in candidates:
            more = min(most - counts[i], max(1, remaining * portions[i] // mass), spare)
            counts[i] = counts[i] + more
            spare = spare - more
    return np.array([most] + counts)


def ragged_sizes(key, count, total, most, lean):
    if count == 2:
        one = jax.random.randint(key, (), max(1, total - most), min(most, total - 1) + 1)
        return jnp.stack([one, total - one])
    tallies = jnp.asarray(profile(count, total, most, lean), jnp.int32)
    couples = (count - 1) // 2
    source_of, receiver = tallies[1:1 + 2 * couples:2], tallies[2:2 + 2 * couples:2]
    margin = jnp.minimum(source_of - 1, most - receiver)
    shifted = jax.random.randint(jax.random.fold_in(key, 1), (couples,), 0, 1 << 20) % (margin + 1)
    tallies = tallies.at[1:1 + 2 * couples:2].set(source_of - shifted).at[2:2 + 2 * couples:2].set(receiver + shifted)
    return tallies[jax.random.permutation(jax.random.fold_in(key, 2), count)]


def gaussian(own_key, shape, scale, limit, shards=(), kind=jnp.bfloat16):
    factor_of = block_levels(own_key, shape, shards, -0.22, 0.18) if shards else 1.0
    values = jax.random.normal(own_key, shape, jnp.float32) * scale * factor_of
    return jnp.minimum(jnp.maximum(values, -limit), limit).astype(kind)


def setup_inputs(seed: int = 0) -> dict:
    key_list = jax.random.split(jax.random.key(seed), 9)
    return {
        "inputs": draw_inputs(jax.random.fold_in(key_list[8], 71), 0),
        "grad_output": gaussian(key_list[1], (BATCH, SEQ, D), 1.0, 6.0, ((0, 16), (1, 32))),
        "query_weight": draw_query_weight(jax.random.fold_in(key_list[8], 71), 0),
        "key_weight": draw_key_weight(jax.random.fold_in(key_list[8], 71), 0),
        "value_weight": gaussian(key_list[4], (D, HD), D ** -0.5, 0.09375, ((0, 32),)),
        "out_weight": gaussian(key_list[5], (HEADS * HD, D), (HEADS * HD) ** -0.5, 0.25, ((1, 32),)),
        "doc_lengths": jax.vmap(lambda own: ragged_sizes(own, NDOC, SEQ, MAXDOC, 2))(jax.random.split(key_list[6], BATCH)).reshape((BATCH, NDOC)).astype(jnp.int32),
        "block_order": jax.vmap(lambda own: jax.random.permutation(own, NBLK))(jax.random.split(key_list[7], BATCH)).reshape((BATCH, NBLK)).astype(jnp.int32),
    }


THETA = 500000.0
NEG = -1e30


def angles(positions, head_size):
    half_width = head_size // 2
    frequency = jnp.exp(-jnp.log(jnp.float32(THETA)) * (2.0 * jnp.arange(half_width, dtype=jnp.float32) / head_size))
    phases = positions.astype(jnp.float32)[:, None] * frequency[None, :]
    return jnp.cos(phases), jnp.sin(phases)


def rotate(vectors, cosine_table, sine_table):
    half_width = vectors.shape[-1] // 2
    first_half = vectors[..., :half_width]
    second_half = vectors[..., half_width:]
    return jnp.concatenate([first_half * cosine_table - second_half * sine_table,
                            second_half * cosine_table + first_half * sine_table], axis=-1)


def layout(order, lengths, total_rows):
    block_width = total_rows // order.shape[0]
    positions = jnp.repeat(order * block_width, block_width, total_repeat_length=total_rows) + jnp.tile(
        jnp.arange(block_width, dtype=jnp.int32), order.shape[0])
    doc_ends = jnp.cumsum(lengths).astype(jnp.int32)
    documents = jnp.sum((positions[:, None] >= doc_ends[None, :]).astype(jnp.int32), axis=1)
    return positions.astype(jnp.int32), documents


def one_sequence(tokens, upstream, order, lengths, query_weight, key_weight, value_weight, out_weight):
    total_rows = tokens.shape[0]
    positions, documents = layout(order, lengths, total_rows)
    cosine_table, sine_table = angles(positions, HD)
    head_cosine = cosine_table[:, None, :]
    head_sine = sine_table[:, None, :]
    queries = rotate(jnp.dot(tokens, query_weight, preferred_element_type=jnp.float32).reshape(total_rows, HEADS, HD),
                     head_cosine, head_sine).astype(jnp.bfloat16)
    rotated_keys = rotate(jnp.dot(tokens, key_weight, preferred_element_type=jnp.float32),
                          cosine_table, sine_table).astype(jnp.bfloat16)
    all_values = jnp.dot(tokens, value_weight, preferred_element_type=jnp.float32).astype(jnp.bfloat16)
    allowed = (documents[:, None] == documents[None, :]) & (positions[None, :] <= positions[:, None])
    scaling = HD ** -0.5
    scores = jnp.einsum("thd,kd->htk", queries.astype(jnp.float32), rotated_keys.astype(jnp.float32)) * scaling
    masked = jnp.where(allowed[None], scores, NEG)
    running_max = jnp.max(masked, axis=2)
    running_sum = jnp.sum(jnp.where(allowed[None], jnp.exp(masked - running_max[:, :, None]), 0.0), axis=2)
    log_total = running_max + jnp.log(running_sum)
    weights = jnp.where(allowed[None], jnp.exp(masked - log_total[:, :, None]), 0.0)
    probabilities = weights.astype(jnp.bfloat16)
    attention = jnp.einsum("htk,kd->thd", probabilities.astype(jnp.float32),
                           all_values.astype(jnp.float32)).astype(jnp.bfloat16)
    grad_attention = jnp.dot(upstream, out_weight.T, preferred_element_type=jnp.float32).astype(
        jnp.bfloat16).reshape(total_rows, HEADS, HD)
    correction = jnp.einsum("thd,thd->ht", grad_attention.astype(jnp.float32), attention.astype(jnp.float32))
    grad_prob = jnp.einsum("thd,kd->htk", grad_attention.astype(jnp.float32), all_values.astype(jnp.float32))
    grad_score = (weights * (grad_prob - correction[:, :, None]) * scaling).astype(jnp.bfloat16)
    grad_query_rot = jnp.einsum("htk,kd->thd", grad_score.astype(jnp.float32), rotated_keys.astype(jnp.float32))
    grad_query = rotate(grad_query_rot, head_cosine, -head_sine).astype(jnp.bfloat16).reshape(total_rows, HEADS * HD)
    score_groups = grad_score.astype(jnp.float32).reshape(HEADS, N_CTX, TOK_DEV, total_rows)
    prob_groups = probabilities.astype(jnp.float32).reshape(HEADS, N_CTX, TOK_DEV, total_rows)
    query_groups = queries.astype(jnp.float32).reshape(N_CTX, TOK_DEV, HEADS, HD)
    attention_groups = grad_attention.astype(jnp.float32).reshape(N_CTX, TOK_DEV, HEADS, HD)
    key_terms = jnp.einsum("hgtk,gthd->gkd", score_groups, query_groups)
    value_terms = jnp.einsum("hgtk,gthd->gkd", prob_groups, attention_groups)
    pair_terms = jnp.concatenate([key_terms, value_terms], axis=2).astype(jnp.bfloat16)
    pair_sum = jnp.sum(lax.optimization_barrier(pair_terms).astype(jnp.float32), axis=0)
    grad_key = rotate(pair_sum[:, :HD], cosine_table, -sine_table).astype(jnp.bfloat16)
    grad_value = pair_sum[:, HD:].astype(jnp.bfloat16)
    grad_input = (jnp.dot(grad_query, query_weight.T, preferred_element_type=jnp.float32)
                  + jnp.dot(grad_key, key_weight.T, preferred_element_type=jnp.float32)
                  + jnp.dot(grad_value, value_weight.T, preferred_element_type=jnp.float32)).astype(jnp.bfloat16)
    weight_part = jnp.dot(tokens.T, grad_value, preferred_element_type=jnp.float32)
    return grad_input, weight_part


def reference(inputs, grad_output, query_weight, key_weight, value_weight, out_weight, doc_lengths, block_order):
    def single(packed):
        return one_sequence(packed[0], packed[1], packed[2], packed[3],
                            query_weight, key_weight, value_weight, out_weight)

    grad_input, weight_parts = lax.map(single, (inputs, grad_output, block_order, doc_lengths))
    return grad_input, jnp.sum(weight_parts, axis=0)
```

```python
import math

import jax
import jax.numpy as jnp
from jax import lax
from jax.experimental import pallas as pl
from jax.experimental.pallas import tpu as pltpu
from jax.sharding import PartitionSpec as P

THETA = 500000.0
NEG = -1e30
BLOCK = 64
LONGEST = 1024
BF16 = jnp.bfloat16
F32 = jnp.float32
NT = (((1,), (1,)), ((), ()))
TN = (((0,), (0,)), ((), ()))
NN = (((1,), (0,)), ((), ()))
VMEM = pl.BlockSpec(memory_space=pltpu.VMEM)
SMEM = pl.BlockSpec(memory_space=pltpu.SMEM)


def call(body, outs, in_specs, args, flops, scratch=(), limit=48):
    moved = sum(math.prod(a.shape) * a.dtype.itemsize for a in list(args) + list(outs))
    return pl.pallas_call(
        body,
        out_shape=outs,
        in_specs=in_specs,
        out_specs=[VMEM] * len(outs),
        scratch_shapes=list(scratch),
        compiler_params=pltpu.CompilerParams(vmem_limit_bytes=limit << 20),
        cost_estimate=pl.CostEstimate(flops=flops, bytes_accessed=moved, transcendentals=0),
    )(*args)


def shape(dims, dtype=BF16):
    return jax.ShapeDtypeStruct(dims, dtype)


def tables(block_numbers, head_size):
    half = head_size // 2
    frequency = jnp.exp(-jnp.log(jnp.float32(THETA)) * (2.0 * jnp.arange(half, dtype=F32) / head_size))
    places = (block_numbers[:, None] * BLOCK + jnp.arange(BLOCK, dtype=jnp.int32)[None, :]).reshape(-1)
    phases = places.astype(F32)[:, None] * frequency[None, :]
    cosine, sine = jnp.cos(phases), jnp.sin(phases)
    return jnp.concatenate([cosine, cosine], 1), jnp.concatenate([-sine, sine], 1)


def swap_halves(v):
    return pltpu.roll(v, v.shape[-1] // 2, axis=1)


def project_kernel(tokens, weight, cosine, sine, out):
    v = lax.dot_general(tokens[...], weight[...], NN, preferred_element_type=F32)
    v = (v * cosine[...] + swap_halves(v) * sine[...]).astype(BF16)
    for chip in range(out.shape[0]):
        out[chip] = v


def attention_kernel(place, order, lengths, tokens, upstream, weights, keys_values, cosine, sine,
                     grad_query, kept, sent, q_ref, a_ref, key_window, value_window, total, stored_at):
    rows, features = tokens.shape
    head = cosine.shape[1]
    heads = q_ref.shape[1] // head
    seq = keys_values.shape[1]
    blocks = seq // BLOCK
    span = key_window.shape[0] // BLOCK
    scaling = head ** (-0.5)
    own = place[0]
    own_core = own % 2

    def invert(i, carry):
        stored_at[order[0, i]] = i
        return carry

    lax.fori_loop(0, blocks, invert, 0)
    width = heads * head
    queries = lax.dot_general(tokens[...], weights[:, :width], NN, preferred_element_type=F32)
    c, s = cosine[...], sine[...]
    for h in range(heads):
        v = queries[:, h * head:(h + 1) * head]
        q_ref[:, h * head:(h + 1) * head] = (v * c + swap_halves(v) * s).astype(BF16)
    a_ref[...] = lax.dot_general(upstream[...], weights[:, width:], NN, preferred_element_type=F32).astype(BF16)
    total[...] = jnp.zeros_like(total)

    def destination(kb):
        spot = stored_at[jnp.maximum(kb, 0)]
        device = spot // 2
        away = jnp.where(device % 2 == own_core, 0, seq // 2)
        return pl.multiple_of(away + (device // 2) * (2 * BLOCK) + (spot % 2) * BLOCK, BLOCK)

    for j in range(rows // BLOCK):
        r0 = j * BLOCK
        block = order[0, own * (rows // BLOCK) + j]
        first = block - (span - 1)
        for w in range(span):
            source = pl.multiple_of(stored_at[jnp.maximum(first + w, 0)] * BLOCK, BLOCK)
            key_window[w * BLOCK:(w + 1) * BLOCK, :] = keys_values[0, pl.ds(source, BLOCK), :]
            value_window[w * BLOCK:(w + 1) * BLOCK, :] = keys_values[1, pl.ds(source, BLOCK), :]
        q = jnp.concatenate([q_ref[r0:r0 + BLOCK, h * head:(h + 1) * head] for h in range(heads)], 0)
        a = jnp.concatenate([a_ref[r0:r0 + BLOCK, h * head:(h + 1) * head] for h in range(heads)], 0)
        lane = lax.broadcasted_iota(jnp.int32, (1, heads * BLOCK), 1)
        query_place = block * BLOCK + lane % BLOCK
        start = jnp.zeros_like(query_place)
        end = jnp.int32(0)
        for d in range(lengths.shape[1]):
            end = end + lengths[0, d]
            start = jnp.where(query_place >= end, end, start)
        key_place = first * BLOCK + lax.broadcasted_iota(jnp.int32, (span * BLOCK, heads * BLOCK), 0)
        allowed = (key_place >= start) & (key_place <= query_place)
        k, v = key_window[...], value_window[...]
        scores = lax.dot_general(k, q, NT, preferred_element_type=F32) * scaling
        scores = jnp.where(allowed, scores, NEG)
        e = jnp.exp(scores - jnp.max(scores, axis=0, keepdims=True))
        weight = e * (1.0 / jnp.sum(e, axis=0, keepdims=True))
        probability = weight.astype(BF16)
        grad_probability = lax.dot_general(v, a, NT, preferred_element_type=F32)
        correction = jnp.sum(probability.astype(F32) * grad_probability, axis=0, keepdims=True)
        grad_score = (weight * (grad_probability - correction) * scaling).astype(BF16)
        key_part = lax.dot_general(grad_score, q, NN, preferred_element_type=F32)
        value_part = lax.dot_general(probability, a, NN, preferred_element_type=F32)
        for w in range(span):
            to = destination(first + w)
            total[pl.ds(to, BLOCK), :head] += key_part[w * BLOCK:(w + 1) * BLOCK]
            total[pl.ds(to, BLOCK), head:] += value_part[w * BLOCK:(w + 1) * BLOCK]
        g = lax.dot_general(k, grad_score, TN, preferred_element_type=F32).T
        for h in range(heads):
            u = g[h * BLOCK:(h + 1) * BLOCK]
            u = u * c[r0:r0 + BLOCK] - swap_halves(u) * s[r0:r0 + BLOCK]
            grad_query[r0:r0 + BLOCK, h * head:(h + 1) * head] = u.astype(BF16)
    half = seq // 2
    kept[...] = total[:half].astype(BF16)
    sent[...] = total[half:].astype(BF16)


def owner_kernel(place, pieces, tokens, cosine, sine, grad_key_value, kept, sent):
    head = cosine.shape[1]
    total = jnp.sum(pieces[...].astype(F32), axis=0)
    u = total[:, :head]
    grad_key_value[:, :head] = (u * cosine[...] - swap_halves(u) * sine[...]).astype(BF16)
    grad_value = total[:, head:].astype(BF16)
    grad_key_value[:, head:] = grad_value
    rows = tokens.shape[0]
    own_core = place[0] % 2
    for chip in range(tokens.shape[1] // (2 * rows)):
        for away in range(2):
            core = jnp.where(own_core == away, 0, 1)
            columns = pl.ds(pl.multiple_of((2 * chip + core) * rows, rows), rows)
            part = lax.dot_general(tokens[:, columns], grad_value, TN, preferred_element_type=F32)
            (sent if away else kept)[chip * rows:(chip + 1) * rows, :] = part.astype(BF16)


def input_kernel(grad_query, grad_key_value, query_weight, other_weight, out):
    width = grad_query.shape[1]
    out[...] = (
        lax.dot_general(grad_query[...], query_weight[:, :width], NT, preferred_element_type=F32)
        + lax.dot_general(grad_key_value[:, :width // 4], other_weight[0], NT, preferred_element_type=F32)
        + lax.dot_general(grad_key_value[:, width // 4:], other_weight[1], NT, preferred_element_type=F32)
    ).astype(BF16)


def on_device(inputs, grad_output, query_weight, key_weight, value_weight, out_weight, doc_lengths, block_order):
    tokens, upstream = inputs[0], grad_output[0]
    rows, features = tokens.shape
    ctx, dp = lax.axis_size("ctx"), lax.axis_size("dp")
    chips = ctx // 2
    seq = rows * ctx
    me = lax.axis_index("ctx")
    core = me % 2
    head = key_weight.shape[1]
    width = query_weight.shape[1]
    heads = width // head
    cores = [[2 * i, 2 * i + 1] for i in range(chips)]
    planes = [[2 * i + c for i in range(chips)] for c in range(2)]
    other = [(i, i ^ 1) for i in range(ctx)]
    place = me.astype(jnp.int32).reshape(1)

    def to_chips(pieces):
        return lax.all_to_all(pieces, "ctx", 0, 0, tiled=True, axis_index_groups=planes)

    packed = jnp.concatenate([query_weight, out_weight.T], axis=1)
    big_weights = lax.all_gather(packed, "ctx", axis=0, tiled=True)

    chip_blocks = lax.dynamic_slice_in_dim(block_order[0], (me // 2) * 4, 4)
    chip_cosine, chip_sine = tables(chip_blocks, head)
    cosine = lax.dynamic_slice_in_dim(chip_cosine, core * rows, rows)
    sine = lax.dynamic_slice_in_dim(chip_sine, core * rows, rows)
    is_key = core == 0
    own_cosine = jnp.where(is_key, chip_cosine, 1.0)
    own_sine = jnp.where(is_key, chip_sine, 0.0)

    chip_tokens = lax.all_gather(tokens, "ctx", axis=0, tiled=True, axis_index_groups=cores)
    both = lax.all_gather(jnp.stack([key_weight, value_weight]), "ctx", axis=1, tiled=True, axis_index_groups=cores)
    mine = lax.dynamic_index_in_dim(both, core, 0, keepdims=False)
    own_weight = to_chips(jnp.broadcast_to(mine[None], (chips,) + mine.shape)).reshape(features, head)
    (projected,) = call(
        project_kernel, [shape((chips, 2 * rows, head))], [VMEM] * 4,
        (chip_tokens, own_weight, own_cosine, own_sine), 4 * rows * features * head)
    own_part = to_chips(projected).reshape(1, seq, head)
    keys_values = lax.all_gather(own_part, "ctx", axis=0, tiled=True, axis_index_groups=cores)
    other_weight = lax.all_gather(own_weight[None], "ctx", axis=0, tiled=True, axis_index_groups=cores)

    window = LONGEST + 2 * BLOCK
    grad_query, kept, sent = call(
        attention_kernel,
        [shape((rows, width)), shape((seq // 2, 2 * head)), shape((seq // 2, 2 * head))],
        [SMEM] * 3 + [VMEM] * 6,
        (place, block_order, doc_lengths, tokens, upstream, big_weights, keys_values, cosine, sine),
        4 * rows * features * width + 20 * rows * heads * window * head,
        scratch=[pltpu.VMEM((rows, width), BF16), pltpu.VMEM((rows, width), BF16),
                 pltpu.VMEM((window, head), BF16), pltpu.VMEM((window, head), BF16),
                 pltpu.VMEM((seq, 2 * head), F32), pltpu.SMEM((seq // BLOCK,), jnp.int32)])
    pairs = (kept.astype(F32) + lax.ppermute(sent, "ctx", other).astype(F32)).astype(BF16)
    pieces = to_chips(pairs).reshape(chips, rows, 2 * head)
    grad_key_value, kept, sent = call(
        owner_kernel,
        [shape((rows, 2 * head)), shape((features // 2, head)), shape((features // 2, head))],
        [SMEM] + [VMEM] * 4, (place, pieces, tokens, cosine, sine), 2 * rows * features * head)
    received = lax.ppermute(sent, "ctx", other)
    (grad_input,) = call(
        input_kernel, [shape((rows, features))], [VMEM] * 4,
        (grad_query, grad_key_value, big_weights, other_weight), 2 * rows * features * (width + 2 * head))
    parts = (kept.astype(F32) + received.astype(F32)).astype(BF16)
    shard = jnp.sum(to_chips(parts).reshape(chips, rows, head).astype(F32), axis=0).astype(BF16)
    slices = lax.all_to_all(shard, "dp", 0, 0, tiled=True).reshape(dp, rows // dp, head)
    own_slice = jnp.sum(slices.astype(F32), axis=0)
    grad_weight = lax.all_to_all(
        jnp.broadcast_to(own_slice[None], (dp,) + own_slice.shape), "dp", 0, 0, tiled=True).reshape(rows, head)
    return grad_input[None], grad_weight


def solution(mesh):
    placed = (
        P("dp", "ctx", None),
        P("dp", "ctx", None),
        P("ctx", None),
        P("ctx", None),
        P("ctx", None),
        P(None, "ctx"),
        P("dp", None),
        P("dp", None),
    )
    return jax.shard_map(
        on_device,
        mesh=mesh,
        in_specs=placed,
        out_specs=(P("dp", "ctx", None), P("ctx", None)),
        check_vma=False,
    )
```

```python
import math

import jax
import jax.numpy as jnp
from jax import lax
from jax.experimental import pallas as pl
from jax.experimental.pallas import tpu as pltpu
from jax.sharding import PartitionSpec as P

THETA = 500000.0
NEG = -1e30
BLOCK = 64
LONGEST = 1024
BF16 = jnp.bfloat16
F32 = jnp.float32
NT = (((1,), (1,)), ((), ()))
TN = (((0,), (0,)), ((), ()))
NN = (((1,), (0,)), ((), ()))
VMEM = pl.BlockSpec(memory_space=pltpu.VMEM)
SMEM = pl.BlockSpec(memory_space=pltpu.SMEM)


def call(body, outs, in_specs, args, flops, scratch=(), limit=48):
    moved = sum(math.prod(a.shape) * a.dtype.itemsize for a in list(args) + list(outs))
    return pl.pallas_call(
        body,
        out_shape=outs,
        in_specs=in_specs,
        out_specs=[VMEM] * len(outs),
        scratch_shapes=list(scratch),
        compiler_params=pltpu.CompilerParams(vmem_limit_bytes=limit << 20),
        cost_estimate=pl.CostEstimate(flops=flops, bytes_accessed=moved, transcendentals=0),
    )(*args)


def shape(dims, dtype=BF16):
    return jax.ShapeDtypeStruct(dims, dtype)


def tables(block_numbers, head_size):
    half = head_size // 2
    frequency = jnp.exp(-jnp.log(jnp.float32(THETA)) * (2.0 * jnp.arange(half, dtype=F32) / head_size))
    places = (block_numbers[:, None] * BLOCK + jnp.arange(BLOCK, dtype=jnp.int32)[None, :]).reshape(-1)
    phases = places.astype(F32)[:, None] * frequency[None, :]
    cosine, sine = jnp.cos(phases), jnp.sin(phases)
    return jnp.concatenate([cosine, cosine], 1), jnp.concatenate([-sine, sine], 1)


def swap_halves(v):
    return pltpu.roll(v, v.shape[-1] // 2, axis=1)


def project_kernel(place, tokens, other_tokens, weight, cosine, sine, out):
    rows = tokens.shape[0]
    own_core = place[0] % 2
    for source, core in ((tokens, own_core), (other_tokens, 1 - own_core)):
        here = pl.ds(pl.multiple_of(core * rows, rows), rows)
        v = lax.dot_general(source[...], weight[...], NN, preferred_element_type=F32)
        v = (v * cosine[here, :] + swap_halves(v) * sine[here, :]).astype(BF16)
        for chip in range(out.shape[0]):
            out[chip, here, :] = v


def attention_kernel(place, order, lengths, tokens, upstream, weights, own_part, other_part, cosine, sine,
                     grad_query, kept, sent, q_ref, a_ref, key_window, value_window, total, stored_at):
    rows, features = tokens.shape
    head = cosine.shape[1]
    heads = q_ref.shape[1] // head
    seq = own_part.shape[0]
    blocks = seq // BLOCK
    span = key_window.shape[0] // BLOCK
    scaling = head ** (-0.5)
    own = place[0]
    own_core = own % 2

    def invert(i, carry):
        stored_at[order[0, i]] = i
        return carry

    lax.fori_loop(0, blocks, invert, 0)
    width = heads * head
    queries = lax.dot_general(tokens[...], weights[:, :width], NN, preferred_element_type=F32)
    c, s = cosine[...], sine[...]
    for h in range(heads):
        v = queries[:, h * head:(h + 1) * head]
        q_ref[:, h * head:(h + 1) * head] = (v * c + swap_halves(v) * s).astype(BF16)
    a_ref[...] = lax.dot_general(upstream[...], weights[:, width:], NN, preferred_element_type=F32).astype(BF16)
    total[...] = jnp.zeros_like(total)

    def destination(kb):
        spot = stored_at[jnp.maximum(kb, 0)]
        device = spot // 2
        away = jnp.where(device % 2 == own_core, 0, seq // 2)
        return pl.multiple_of(away + (device // 2) * (2 * BLOCK) + (spot % 2) * BLOCK, BLOCK)

    for j in range(rows // BLOCK):
        r0 = j * BLOCK
        block = order[0, own * (rows // BLOCK) + j]
        first = block - (span - 1)
        for w in range(span):
            source = pl.multiple_of(stored_at[jnp.maximum(first + w, 0)] * BLOCK, BLOCK)
            first_half, second_half = own_part[pl.ds(source, BLOCK), :], other_part[pl.ds(source, BLOCK), :]
            key_window[w * BLOCK:(w + 1) * BLOCK, :] = jnp.where(own_core == 0, first_half, second_half)
            value_window[w * BLOCK:(w + 1) * BLOCK, :] = jnp.where(own_core == 0, second_half, first_half)
        q = jnp.concatenate([q_ref[r0:r0 + BLOCK, h * head:(h + 1) * head] for h in range(heads)], 0)
        a = jnp.concatenate([a_ref[r0:r0 + BLOCK, h * head:(h + 1) * head] for h in range(heads)], 0)
        lane = lax.broadcasted_iota(jnp.int32, (1, heads * BLOCK), 1)
        query_place = block * BLOCK + lane % BLOCK
        start = jnp.zeros_like(query_place)
        end = jnp.int32(0)
        for d in range(lengths.shape[1]):
            end = end + lengths[0, d]
            start = jnp.where(query_place >= end, end, start)
        key_place = first * BLOCK + lax.broadcasted_iota(jnp.int32, (span * BLOCK, heads * BLOCK), 0)
        allowed = (key_place >= start) & (key_place <= query_place)
        k, v = key_window[...], value_window[...]
        scores = lax.dot_general(k, q, NT, preferred_element_type=F32) * scaling
        scores = jnp.where(allowed, scores, NEG)
        e = jnp.exp(scores - jnp.max(scores, axis=0, keepdims=True))
        weight = e * (1.0 / jnp.sum(e, axis=0, keepdims=True))
        probability = weight.astype(BF16)
        grad_probability = lax.dot_general(v, a, NT, preferred_element_type=F32)
        correction = jnp.sum(probability.astype(F32) * grad_probability, axis=0, keepdims=True)
        grad_score = (weight * (grad_probability - correction) * scaling).astype(BF16)
        key_part = lax.dot_general(grad_score, q, NN, preferred_element_type=F32)
        value_part = lax.dot_general(probability, a, NN, preferred_element_type=F32)
        for w in range(span):
            to = destination(first + w)
            total[pl.ds(to, BLOCK), :head] += key_part[w * BLOCK:(w + 1) * BLOCK]
            total[pl.ds(to, BLOCK), head:] += value_part[w * BLOCK:(w + 1) * BLOCK]
        g = lax.dot_general(k, grad_score, TN, preferred_element_type=F32).T
        for h in range(heads):
            u = g[h * BLOCK:(h + 1) * BLOCK]
            u = u * c[r0:r0 + BLOCK] - swap_halves(u) * s[r0:r0 + BLOCK]
            grad_query[r0:r0 + BLOCK, h * head:(h + 1) * head] = u.astype(BF16)
    half = seq // 2
    kept[...] = total[:half].astype(BF16)
    sent[...] = total[half:].astype(BF16)


def owner_kernel(place, pieces, tokens, cosine, sine, grad_key_value, kept, sent):
    head = cosine.shape[1]
    total = jnp.sum(pieces[...].astype(F32), axis=0)
    u = total[:, :head]
    grad_key_value[:, :head] = (u * cosine[...] - swap_halves(u) * sine[...]).astype(BF16)
    grad_value = total[:, head:].astype(BF16)
    grad_key_value[:, head:] = grad_value
    rows = tokens.shape[0]
    own_core = place[0] % 2
    for chip in range(tokens.shape[1] // (2 * rows)):
        for away in range(2):
            core = jnp.where(own_core == away, 0, 1)
            columns = pl.ds(pl.multiple_of((2 * chip + core) * rows, rows), rows)
            part = lax.dot_general(tokens[:, columns], grad_value, TN, preferred_element_type=F32)
            (sent if away else kept)[chip * rows:(chip + 1) * rows, :] = part.astype(BF16)


def input_kernel(place, grad_query, grad_key_value, query_weight, own_weight, other_weight, out):
    width = grad_query.shape[1]
    head = own_weight.shape[1]
    own_core = place[0] % 2
    grad_key, grad_value = grad_key_value[:, :head], grad_key_value[:, head:]
    own_grad = jnp.where(own_core == 0, grad_key, grad_value)
    other_grad = jnp.where(own_core == 0, grad_value, grad_key)
    out[...] = (
        lax.dot_general(grad_query[...], query_weight[:, :width], NT, preferred_element_type=F32)
        + lax.dot_general(own_grad, own_weight[...], NT, preferred_element_type=F32)
        + lax.dot_general(other_grad, other_weight[...], NT, preferred_element_type=F32)
    ).astype(BF16)


def on_device(inputs, grad_output, query_weight, key_weight, value_weight, out_weight, doc_lengths, block_order):
    tokens, upstream = inputs[0], grad_output[0]
    rows, features = tokens.shape
    ctx, dp = lax.axis_size("ctx"), lax.axis_size("dp")
    chips = ctx // 2
    seq = rows * ctx
    me = lax.axis_index("ctx")
    core = me % 2
    head = key_weight.shape[1]
    width = query_weight.shape[1]
    heads = width // head
    planes = [[2 * i + c for i in range(chips)] for c in range(2)]
    other = [(i, i ^ 1) for i in range(ctx)]
    place = me.astype(jnp.int32).reshape(1)

    def to_chips(pieces):
        return lax.all_to_all(pieces, "ctx", 0, 0, tiled=True, axis_index_groups=planes)

    packed = jnp.concatenate([query_weight, out_weight.T], axis=1)
    big_weights = lax.all_gather(packed, "ctx", axis=0, tiled=True)

    chip_blocks = lax.dynamic_slice_in_dim(block_order[0], (me // 2) * 4, 4)
    chip_cosine, chip_sine = tables(chip_blocks, head)
    cosine = lax.dynamic_slice_in_dim(chip_cosine, core * rows, rows)
    sine = lax.dynamic_slice_in_dim(chip_sine, core * rows, rows)
    is_key = core == 0
    own_cosine = jnp.where(is_key, chip_cosine, 1.0)
    own_sine = jnp.where(is_key, chip_sine, 0.0)

    def swap(v):
        return lax.ppermute(v, "ctx", other)

    mine = jnp.where(is_key, key_weight, value_weight)
    theirs = swap(jnp.where(is_key, value_weight, key_weight))
    chip_weight = jnp.concatenate([jnp.where(is_key, mine, theirs), jnp.where(is_key, theirs, mine)], axis=0)
    own_weight = to_chips(
        jnp.broadcast_to(chip_weight[None], (chips,) + chip_weight.shape)).reshape(features, head)
    (projected,) = call(
        project_kernel, [shape((chips, 2 * rows, head))], [SMEM] + [VMEM] * 5,
        (place, tokens, swap(tokens), own_weight, own_cosine, own_sine), 4 * rows * features * head)
    own_part = to_chips(projected).reshape(seq, head)
    other_part = swap(own_part)
    other_weight = swap(own_weight)

    window = LONGEST + 2 * BLOCK
    grad_query, kept, sent = call(
        attention_kernel,
        [shape((rows, width)), shape((seq // 2, 2 * head)), shape((seq // 2, 2 * head))],
        [SMEM] * 3 + [VMEM] * 7,
        (place, block_order, doc_lengths, tokens, upstream, big_weights, own_part, other_part, cosine, sine),
        4 * rows * features * width + 20 * rows * heads * window * head,
        scratch=[pltpu.VMEM((rows, width), BF16), pltpu.VMEM((rows, width), BF16),
                 pltpu.VMEM((window, head), BF16), pltpu.VMEM((window, head), BF16),
                 pltpu.VMEM((seq, 2 * head), F32), pltpu.SMEM((seq // BLOCK,), jnp.int32)])
    pairs = (kept.astype(F32) + swap(sent).astype(F32)).astype(BF16)
    pieces = to_chips(pairs).reshape(chips, rows, 2 * head)
    grad_key_value, kept, sent = call(
        owner_kernel,
        [shape((rows, 2 * head)), shape((features // 2, head)), shape((features // 2, head))],
        [SMEM] + [VMEM] * 4, (place, pieces, tokens, cosine, sine), 2 * rows * features * head)
    received = swap(sent)
    (grad_input,) = call(
        input_kernel, [shape((rows, features))], [SMEM] + [VMEM] * 5,
        (place, grad_query, grad_key_value, big_weights, own_weight, other_weight), 2 * rows * features * (width + 2 * head))
    parts = (kept.astype(F32) + received.astype(F32)).astype(BF16)
    shard = jnp.sum(to_chips(parts).reshape(chips, rows, head).astype(F32), axis=0).astype(BF16)
    slices = lax.all_to_all(shard, "dp", 0, 0, tiled=True).reshape(dp, rows // dp, head)
    own_slice = jnp.sum(slices.astype(F32), axis=0)
    grad_weight = lax.all_to_all(
        jnp.broadcast_to(own_slice[None], (dp,) + own_slice.shape), "dp", 0, 0, tiled=True).reshape(rows, head)
    return grad_input[None], grad_weight


def solution(mesh):
    placed = (
        P("dp", "ctx", None),
        P("dp", "ctx", None),
        P("ctx", None),
        P("ctx", None),
        P("ctx", None),
        P(None, "ctx"),
        P("dp", None),
        P("dp", None),
    )
    return jax.shard_map(
        on_device,
        mesh=mesh,
        in_specs=placed,
        out_specs=(P("dp", "ctx", None), P("ctx", None)),
        check_vma=False,
    )
```

```python
import functools
import math

import jax
import jax.numpy as jnp
from jax import lax
from jax.experimental import pallas as pl
from jax.experimental.pallas import tpu as pltpu
from jax.sharding import PartitionSpec as P

THETA = 500000.0
NEG = -1e30
BLOCK = 64
LONGEST = 1024
RING = (0, -1, 1, 2)
BF16 = jnp.bfloat16
F32 = jnp.float32
NT = (((1,), (1,)), ((), ()))
TN = (((0,), (0,)), ((), ()))
NN = (((1,), (0,)), ((), ()))
VMEM = pl.BlockSpec(memory_space=pltpu.VMEM)
SMEM = pl.BlockSpec(memory_space=pltpu.SMEM)
HBM = pl.BlockSpec(memory_space=pltpu.HBM)


def call(body, outs, in_specs, args, flops, scratch=(), limit=24):
    moved = sum(math.prod(a.shape) * a.dtype.itemsize for a in list(args) + list(outs))
    return pl.pallas_call(
        body,
        out_shape=outs,
        in_specs=in_specs,
        out_specs=[VMEM] * len(outs),
        scratch_shapes=list(scratch),
        compiler_params=pltpu.CompilerParams(vmem_limit_bytes=limit << 20),
        cost_estimate=pl.CostEstimate(flops=flops, bytes_accessed=moved, transcendentals=0),
    )(*args)


def shape(dims, dtype=BF16):
    return jax.ShapeDtypeStruct(dims, dtype)


def tables(block_numbers, head_size):
    half = head_size // 2
    frequency = jnp.exp(-jnp.log(jnp.float32(THETA)) * (2.0 * jnp.arange(half, dtype=F32) / head_size))
    places = (block_numbers[:, None] * BLOCK + jnp.arange(BLOCK, dtype=jnp.int32)[None, :]).reshape(-1)
    phases = places.astype(F32)[:, None] * frequency[None, :]
    cosine, sine = jnp.cos(phases), jnp.sin(phases)
    return jnp.concatenate([cosine, cosine], 1), jnp.concatenate([-sine, sine], 1)


def swap_halves(v):
    return pltpu.roll(v, v.shape[-1] // 2, axis=1)


def fetch(sources, targets, arrived):
    copies = [pltpu.make_async_copy(a, b, arrived.at[i]) for i, (a, b) in enumerate(zip(sources, targets))]
    for copy in copies:
        copy.start()
    return copies


def pack_kernel(query_weight, out_weight, out, query, turned, arrived):
    width = query_weight.shape[1]
    copies = fetch((query_weight, out_weight), (query, turned), arrived)
    copies[0].wait()
    for copy in range(out.shape[0]):
        out[copy, :, :width] = query[...]
    copies[1].wait()
    columns = turned[...].T
    for copy in range(out.shape[0]):
        out[copy, :, width:] = columns


def shard_order(core, chip, side):
    row, column = chip // side, chip % side
    order = []
    for offset in RING:
        for first in range(side):
            down = jnp.where(core == 0, (row + offset + side) % side, first)
            along = jnp.where(core == 0, first, (column + offset + side) % side)
            order.append((down * side + along) * 2 + core)
    return order


def partial_kernel(place, tokens, other_tokens, upstream, other_upstream, *rest, begin):
    pieces, (mine, theirs) = rest[:-2], rest[-2:]
    added = pieces[-2:] if begin else ()
    pieces = pieces[:-2] if begin else pieces
    rows, features = tokens.shape
    width = mine.shape[1] // 2
    side = math.isqrt(features // (2 * rows))
    shards = shard_order(place[0] % 2, place[0] // 2, side)
    for source, start, which, out in ((other_tokens, 0, 1, theirs), (other_upstream, width, 1, theirs),
                                      (tokens, 0, 0, mine), (upstream, width, 0, mine)):
        total = added[which][:, start:start + width] if begin else jnp.zeros((rows, width), F32)
        for n in range(0, side * len(pieces), 2):
            piece, at = pieces[n // side], (n % side) * rows
            columns = [pl.ds(pl.multiple_of(shards[begin * side + n + i] * rows, rows), rows) for i in range(2)]
            t = jnp.concatenate([source[:, here] for here in columns], axis=1)
            total += lax.dot_general(t, piece[at:at + 2 * rows, start:start + width], NN,
                                     preferred_element_type=F32)
        out[:, start:start + width] = total


def project_kernel(place, tokens, other_tokens, weight, cosine, sine, out):
    rows = tokens.shape[0]
    own_core = place[0] % 2
    for source, core in ((tokens, own_core), (other_tokens, 1 - own_core)):
        here = pl.ds(pl.multiple_of(core * rows, rows), rows)
        v = lax.dot_general(source[...], weight[...], NN, preferred_element_type=F32)
        v = (v * cosine[here, :] + swap_halves(v) * sine[here, :]).astype(BF16)
        for chip in range(out.shape[0]):
            out[chip, here, :] = v


def attention_kernel(place, order, lengths, mine_at, theirs_at, own_at, other_at, cosine, sine,
                     grad_query, kept, sent, q_ref, a_ref, key_window, value_window, total, stored_at,
                     mine, theirs, own_part, other_part, arrived):
    copies = fetch((mine_at, theirs_at, own_at, other_at), (mine, theirs, own_part, other_part), arrived)
    rows = mine.shape[0]
    head = cosine.shape[1]
    heads = q_ref.shape[1] // head
    seq = own_part.shape[0]
    blocks = seq // BLOCK
    span = key_window.shape[0] // BLOCK
    scaling = head ** (-0.5)
    own = place[0]
    own_core = own % 2

    def invert(i, carry):
        stored_at[order[0, i]] = i
        return carry

    lax.fori_loop(0, blocks, invert, 0)
    width = heads * head
    total[...] = jnp.zeros_like(total)
    for copy in copies:
        copy.wait()
    queries = mine[:, :width] + theirs[:, :width]
    c, s = cosine[...], sine[...]
    for h in range(heads):
        v = queries[:, h * head:(h + 1) * head]
        q_ref[:, h * head:(h + 1) * head] = (v * c + swap_halves(v) * s).astype(BF16)
    a_ref[...] = (mine[:, width:] + theirs[:, width:]).astype(BF16)

    def destination(kb):
        spot = stored_at[jnp.maximum(kb, 0)]
        device = spot // 2
        away = jnp.where(device % 2 == own_core, 0, seq // 2)
        return pl.multiple_of(away + (device // 2) * (2 * BLOCK) + (spot % 2) * BLOCK, BLOCK)

    for j in range(rows // BLOCK):
        r0 = j * BLOCK
        block = order[0, own * (rows // BLOCK) + j]
        first = block - (span - 1)
        for w in range(span):
            source = pl.multiple_of(stored_at[jnp.maximum(first + w, 0)] * BLOCK, BLOCK)
            first_half, second_half = own_part[pl.ds(source, BLOCK), :], other_part[pl.ds(source, BLOCK), :]
            key_window[w * BLOCK:(w + 1) * BLOCK, :] = jnp.where(own_core == 0, first_half, second_half)
            value_window[w * BLOCK:(w + 1) * BLOCK, :] = jnp.where(own_core == 0, second_half, first_half)
        q = jnp.concatenate([q_ref[r0:r0 + BLOCK, h * head:(h + 1) * head] for h in range(heads)], 0)
        a = jnp.concatenate([a_ref[r0:r0 + BLOCK, h * head:(h + 1) * head] for h in range(heads)], 0)
        lane = lax.broadcasted_iota(jnp.int32, (1, heads * BLOCK), 1)
        query_place = block * BLOCK + lane % BLOCK
        start = jnp.zeros_like(query_place)
        end = jnp.int32(0)
        for d in range(lengths.shape[1]):
            end = end + lengths[0, d]
            start = jnp.where(query_place >= end, end, start)
        key_place = first * BLOCK + lax.broadcasted_iota(jnp.int32, (span * BLOCK, heads * BLOCK), 0)
        allowed = (key_place >= start) & (key_place <= query_place)
        k, v = key_window[...], value_window[...]
        scores = lax.dot_general(k, q, NT, preferred_element_type=F32) * scaling
        scores = jnp.where(allowed, scores, NEG)
        e = jnp.exp(scores - jnp.max(scores, axis=0, keepdims=True))
        weight = e * (1.0 / jnp.sum(e, axis=0, keepdims=True))
        probability = weight.astype(BF16)
        grad_probability = lax.dot_general(v, a, NT, preferred_element_type=F32)
        correction = jnp.sum(probability.astype(F32) * grad_probability, axis=0, keepdims=True)
        grad_score = (weight * (grad_probability - correction) * scaling).astype(BF16)
        key_part = lax.dot_general(grad_score, q, NN, preferred_element_type=F32)
        value_part = lax.dot_general(probability, a, NN, preferred_element_type=F32)
        for w in range(span):
            to = destination(first + w)
            total[pl.ds(to, BLOCK), :head] += key_part[w * BLOCK:(w + 1) * BLOCK]
            total[pl.ds(to, BLOCK), head:] += value_part[w * BLOCK:(w + 1) * BLOCK]
        g = lax.dot_general(k, grad_score, TN, preferred_element_type=F32).T
        for h in range(heads):
            u = g[h * BLOCK:(h + 1) * BLOCK]
            u = u * c[r0:r0 + BLOCK] - swap_halves(u) * s[r0:r0 + BLOCK]
            grad_query[r0:r0 + BLOCK, h * head:(h + 1) * head] = u.astype(BF16)
    half = seq // 2
    kept[...] = total[:half].astype(BF16)
    sent[...] = total[half:].astype(BF16)


def owner_kernel(pieces, cosine, sine, grad_key_value):
    head = cosine.shape[1]
    total = jnp.sum(pieces[...].astype(F32), axis=0)
    u = total[:, :head]
    grad_key_value[:, :head] = (u * cosine[...] - swap_halves(u) * sine[...]).astype(BF16)
    grad_key_value[:, head:] = total[:, head:].astype(BF16)


def weight_kernel(place, tokens, other_tokens, grads, other_grads, out):
    rows, features = tokens.shape
    core = place[0] % 2
    head = out.shape[2]
    both = jnp.concatenate([grads[:, head:], other_grads[:, head:]], axis=0)
    for chip in range(features // (2 * rows)):
        here = pl.ds(pl.multiple_of((2 * chip + core) * rows, rows), rows)
        t = jnp.concatenate([tokens[:, here], other_tokens[:, here]], axis=0)
        out[chip] = lax.dot_general(t, both, TN, preferred_element_type=F32).astype(BF16)


def input_kernel(place, grad_query, other_grad_query, grads, other_grads, own_weight, other_weight,
                 w0, w1, w2, w3, mine, theirs):
    rows, width = grad_query.shape
    head = own_weight.shape[1]
    core = place[0] % 2
    side = math.isqrt(own_weight.shape[0] // (2 * rows))
    queries = jnp.concatenate([grad_query[...], other_grad_query[...]], axis=0)
    both = jnp.concatenate([grads[...], other_grads[...]], axis=0)
    own_grad = jnp.where(core == 0, both[:, :head], both[:, head:])
    other_grad = jnp.where(core == 0, both[:, head:], both[:, :head])
    for n, shard in enumerate(shard_order(core, place[0] // 2, side)):
        at = (n % side) * rows
        here = pl.ds(pl.multiple_of(shard * rows, rows), rows)
        to = pl.ds(pl.multiple_of((shard // 2) * rows, rows), rows)
        part = (
            lax.dot_general(queries, (w0, w1, w2, w3)[n // side][at:at + rows, :width], NT,
                            preferred_element_type=F32)
            + lax.dot_general(own_grad, own_weight[here, :], NT, preferred_element_type=F32)
            + lax.dot_general(other_grad, other_weight[here, :], NT, preferred_element_type=F32)
        ).astype(BF16)
        mine[:, to] = part[:rows]
        theirs[:, to] = part[rows:]


def merge_kernel(place, mine, received, out):
    rows = out.shape[0]
    core = place[0] % 2
    for chip in range(mine.shape[1] // rows):
        for source, shard in ((mine, 2 * chip + core), (received, 2 * chip + 1 - core)):
            out[:, pl.ds(pl.multiple_of(shard * rows, rows), rows)] = source[:, chip * rows:(chip + 1) * rows]


def on_device(inputs, grad_output, query_weight, key_weight, value_weight, out_weight, doc_lengths, block_order):
    tokens, upstream = inputs[0], grad_output[0]
    rows, features = tokens.shape
    ctx, dp = lax.axis_size("ctx"), lax.axis_size("dp")
    chips = ctx // 2
    seq = rows * ctx
    me = lax.axis_index("ctx")
    core = me % 2
    head = key_weight.shape[1]
    width = query_weight.shape[1]
    heads = width // head
    planes = [[2 * i + c for i in range(chips)] for c in range(2)]
    other = [(i, i ^ 1) for i in range(ctx)]
    place = me.astype(jnp.int32).reshape(1)

    def to_chips(pieces):
        return lax.all_to_all(pieces, "ctx", 0, 0, tiled=True, axis_index_groups=planes)

    side = math.isqrt(chips)

    def moved(v, phase, step):
        pairs = []
        for row in range(side):
            for column in range(side):
                for c in range(2):
                    to = (row, (column + step) % side) if c == phase else ((row + step) % side, column)
                    pairs.append(((row * side + column) * 2 + c, (to[0] * side + to[1]) * 2 + c))
        return lax.ppermute(v, "ctx", pairs)

    rings = [[(row * side + i) * 2 for i in range(side)] for row in range(side)]
    rings += [[(i * side + column) * 2 + 1 for i in range(side)] for column in range(side)]
    (packed,) = call(pack_kernel, [shape((side, rows, 2 * width))], [HBM] * 2, (query_weight, out_weight), 0,
                     scratch=[pltpu.VMEM((rows, width), BF16), pltpu.VMEM((width, rows), BF16),
                              pltpu.SemaphoreType.DMA((2,))])
    line = lax.all_to_all(packed, "ctx", 0, 0, tiled=True, axis_index_groups=rings).reshape(side * rows, 2 * width)
    held = [line] + [moved(line, 1, -offset) for offset in RING[1:]]

    chip_blocks = lax.dynamic_slice_in_dim(block_order[0], (me // 2) * 4, 4)
    chip_cosine, chip_sine = tables(chip_blocks, head)
    cosine = lax.dynamic_slice_in_dim(chip_cosine, core * rows, rows)
    sine = lax.dynamic_slice_in_dim(chip_sine, core * rows, rows)
    is_key = core == 0
    own_cosine = jnp.where(is_key, chip_cosine, 1.0)
    own_sine = jnp.where(is_key, chip_sine, 0.0)

    def swap(v):
        return lax.ppermute(v, "ctx", other)

    mine = jnp.where(is_key, key_weight, value_weight)
    theirs = swap(jnp.where(is_key, value_weight, key_weight))
    chip_weight = jnp.concatenate([jnp.where(is_key, mine, theirs), jnp.where(is_key, theirs, mine)], axis=0)
    copies, _ = lax.optimization_barrier(
        (jnp.broadcast_to(chip_weight[None], (chips,) + chip_weight.shape), line))
    own_weight = to_chips(copies).reshape(features, head)
    other_tokens = swap(tokens)
    (projected,) = call(
        project_kernel, [shape((chips, 2 * rows, head))], [SMEM] + [VMEM] * 5,
        (place, tokens, other_tokens, own_weight, own_cosine, own_sine), 4 * rows * features * head)
    sources = (place, tokens, other_tokens, upstream, swap(upstream))
    halves = [shape((rows, 2 * width), F32)] * 2
    mine, theirs = call(
        functools.partial(partial_kernel, begin=0), halves, [SMEM] + [VMEM] * 7,
        sources + tuple(held[:3]), 3 * rows * features * width)
    mine, theirs = call(
        functools.partial(partial_kernel, begin=3), halves, [SMEM] + [VMEM] * 7,
        sources + (held[3], mine, theirs), rows * features * width)
    own_part = to_chips(projected).reshape(seq, head)
    own_part, mine, theirs = lax.optimization_barrier((own_part, mine, theirs))
    received = swap(theirs)
    other_part = swap(own_part)
    other_weight = swap(own_weight)
    window = LONGEST + 2 * BLOCK
    grad_query, kept, sent = call(
        attention_kernel,
        [shape((rows, width)), shape((seq // 2, 2 * head)), shape((seq // 2, 2 * head))],
        [SMEM] * 3 + [HBM] * 4 + [VMEM] * 2,
        (place, block_order, doc_lengths, mine, received, own_part, other_part, cosine, sine),
        20 * rows * heads * window * head,
        scratch=[pltpu.VMEM((rows, width), BF16), pltpu.VMEM((rows, width), BF16),
                 pltpu.VMEM((window, head), BF16), pltpu.VMEM((window, head), BF16),
                 pltpu.VMEM((seq, 2 * head), F32), pltpu.SMEM((seq // BLOCK,), jnp.int32),
                 pltpu.VMEM((rows, 2 * width), F32), pltpu.VMEM((rows, 2 * width), F32),
                 pltpu.VMEM((seq, head), BF16), pltpu.VMEM((seq, head), BF16), pltpu.SemaphoreType.DMA((4,))],
        limit=28)
    pairs = (kept.astype(F32) + swap(sent).astype(F32)).astype(BF16)
    pieces = to_chips(pairs).reshape(chips, rows, 2 * head)
    (grads,) = call(owner_kernel, [shape((rows, 2 * head))], [VMEM] * 3, (pieces, cosine, sine), 0)
    other_grads = swap(grads)
    (parts,) = call(
        weight_kernel, [shape((chips, rows, head))], [SMEM] + [VMEM] * 4,
        (place, tokens, other_tokens, grads, other_grads), 2 * rows * features * head)
    input_mine, input_theirs = call(
        input_kernel, [shape((rows, features // 2))] * 2, [SMEM] + [VMEM] * 10,
        (place, grad_query, swap(grad_query), grads, other_grads, own_weight, other_weight, *held),
        2 * rows * features * (width + 2 * head))
    (grad_input,) = call(
        merge_kernel, [shape((rows, features))], [SMEM] + [VMEM] * 2,
        (place, input_mine, swap(input_theirs)), 0)
    grad_weight = jnp.sum(to_chips(parts).reshape(chips, rows, head).astype(F32), axis=0)
    group, step = dp, dp // 2
    while group > 4 and group % 2 == 0:
        sent_on = lax.ppermute(grad_weight.astype(BF16), "dp", [(i, i ^ step) for i in range(dp)])
        grad_weight = grad_weight.astype(BF16).astype(F32) + sent_on.astype(F32)
        group, step = group // 2, step // 2
    near = [[first + i for i in range(group)] for first in range(0, dp, group)]
    spread = jnp.broadcast_to(grad_weight.astype(BF16)[None], (group, rows, head))
    gathered = lax.all_to_all(spread, "dp", 0, 0, tiled=True, axis_index_groups=near)
    grad_weight = jnp.sum(gathered.reshape(group, rows, head).astype(F32), axis=0)
    return grad_input[None], grad_weight


def solution(mesh):
    placed = (
        P("dp", "ctx", None),
        P("dp", "ctx", None),
        P("ctx", None),
        P("ctx", None),
        P("ctx", None),
        P(None, "ctx"),
        P("dp", None),
        P("dp", None),
    )
    return jax.shard_map(
        on_device,
        mesh=mesh,
        in_specs=placed,
        out_specs=(P("dp", "ctx", None), P("ctx", None)),
        check_vma=False,
    )
```

```python
import math

import jax
import jax.numpy as jnp
from jax import lax
from jax.experimental import pallas as pl
from jax.experimental.pallas import tpu as pltpu
from jax.sharding import PartitionSpec as P

THETA = 500000.0
NEG = -1e30
BLOCK = 64
LONGEST = 1024
RING = (0, 2, -1, 1)
BF16 = jnp.bfloat16
F32 = jnp.float32
NT = (((1,), (1,)), ((), ()))
TN = (((0,), (0,)), ((), ()))
NN = (((1,), (0,)), ((), ()))
VMEM = pl.BlockSpec(memory_space=pltpu.VMEM)
SMEM = pl.BlockSpec(memory_space=pltpu.SMEM)
HBM = pl.BlockSpec(memory_space=pltpu.HBM)


def call(body, outs, in_specs, args, flops, scratch=(), limit=24, out_specs=None):
    moved = sum(math.prod(a.shape) * a.dtype.itemsize for a in list(args) + list(outs))
    return pl.pallas_call(
        body,
        out_shape=outs,
        in_specs=in_specs,
        out_specs=out_specs or [VMEM] * len(outs),
        scratch_shapes=list(scratch),
        compiler_params=pltpu.CompilerParams(vmem_limit_bytes=limit << 20),
        cost_estimate=pl.CostEstimate(flops=flops, bytes_accessed=moved, transcendentals=0),
    )(*args)


def shape(dims, dtype=BF16):
    return jax.ShapeDtypeStruct(dims, dtype)


def tables(block_numbers, head_size):
    half = head_size // 2
    frequency = jnp.exp(-jnp.log(jnp.float32(THETA)) * (2.0 * jnp.arange(half, dtype=F32) / head_size))
    places = (block_numbers[:, None] * BLOCK + jnp.arange(BLOCK, dtype=jnp.int32)[None, :]).reshape(-1)
    phases = places.astype(F32)[:, None] * frequency[None, :]
    cosine, sine = jnp.cos(phases), jnp.sin(phases)
    return jnp.concatenate([cosine, cosine], 1), jnp.concatenate([-sine, sine], 1)


def swap_halves(v):
    return pltpu.roll(v, v.shape[-1] // 2, axis=1)


def fetch(sources, targets, arrived):
    copies = [pltpu.make_async_copy(a, b, arrived.at[i]) for i, (a, b) in enumerate(zip(sources, targets))]
    for copy in copies:
        copy.start()
    return copies


def write_copies(source, out, done):
    copies = [pltpu.make_async_copy(source, out.at[i], done.at[i]) for i in range(out.shape[0])]
    for copy in copies:
        copy.start()
    for copy in copies:
        copy.wait()


def pack_kernel(query_weight, out_weight, out, packed, turned, arrived, done):
    width = query_weight.shape[1]
    copies = fetch((query_weight, out_weight), (packed.at[:, :width], turned), arrived)
    copies[1].wait()
    packed[:, width:] = turned[...].T
    copies[0].wait()
    write_copies(packed, out, done)


def spread_kernel(place, key_weight, value_weight, received, out, held, done):
    rows = key_weight.shape[0]
    core = place[0] % 2
    held[pl.ds(pl.multiple_of(core * rows, rows), rows), :] = jnp.where(
        core == 0, key_weight[...], value_weight[...])
    held[pl.ds(pl.multiple_of((1 - core) * rows, rows), rows), :] = received[...]
    write_copies(held, out, done)


def shard_order(core, chip, side):
    row, column = chip // side, chip % side
    order = []
    for offset in RING:
        for first in range(side):
            down = jnp.where(core == 0, (row + offset + side) % side, first)
            along = jnp.where(core == 0, first, (column + offset + side) % side)
            order.append((down * side + along) * 2 + core)
    return order


def partial_sums(place, sources, pieces, added, outs, begin, finished=None):
    rows, features = sources[0].shape
    width = outs[0].shape[1] // 2
    side = math.isqrt(features // (2 * rows))
    shards = shard_order(place[0] % 2, place[0] // 2, side)
    for which in (1, 0):
        for source, start in zip(sources[2 * which:], (0, width)):
            total = added[which][:, start:start + width] if begin else jnp.zeros((rows, width), F32)
            for n in range(0, side * len(pieces), 2):
                piece, at = pieces[n // side], (n % side) * rows
                columns = [pl.ds(pl.multiple_of(shards[begin * side + n + i] * rows, rows), rows) for i in range(2)]
                t = jnp.concatenate([source[:, here] for here in columns], axis=1)
                total += lax.dot_general(t, piece[at:at + 2 * rows, start:start + width], NN,
                                         preferred_element_type=F32)
            outs[which][:, start:start + width] = total
        if which and finished:
            finished()


def first_partial_kernel(place, tokens, upstream, other_tokens, other_upstream, w0, w1, w2, mine, theirs):
    partial_sums(place, (tokens, upstream, other_tokens, other_upstream), (w0, w1, w2), None, (mine, theirs), 0)


def last_partial_kernel(place, tokens, upstream, other_tokens, other_upstream, w3, mine_before, theirs_before,
                        mine, theirs_out, theirs, done):
    copy = pltpu.make_async_copy(theirs, theirs_out, done)
    partial_sums(place, (tokens, upstream, other_tokens, other_upstream), (w3,), (mine_before, theirs_before),
                 (mine, theirs), 3, copy.start)
    copy.wait()


def project_kernel(place, tokens, other_tokens, weight, cosine, sine, out, held, done):
    rows = tokens.shape[0]
    own_core = place[0] % 2
    for source, core in ((tokens, own_core), (other_tokens, 1 - own_core)):
        here = pl.ds(pl.multiple_of(core * rows, rows), rows)
        v = lax.dot_general(source[...], weight[...], NN, preferred_element_type=F32)
        held[here, :] = (v * cosine[here, :] + swap_halves(v) * sine[here, :]).astype(BF16)
    write_copies(held, out, done)


def attention_kernel(place, order, lengths, mine, theirs_at, own_at, other_at, cosine, sine,
                     grad_query, kept, sent, q_ref, a_ref, key_window, value_window, total, stored_at,
                     theirs, own_part, other_part, arrived):
    copies = fetch((theirs_at, own_at, other_at), (theirs, own_part, other_part), arrived)
    rows = mine.shape[0]
    head = cosine.shape[1]
    heads = q_ref.shape[1] // head
    seq = own_part.shape[0]
    blocks = seq // BLOCK
    span = key_window.shape[0] // BLOCK
    scaling = head ** (-0.5)
    own = place[0]
    own_core = own % 2

    def invert(i, carry):
        stored_at[order[0, i]] = i
        return carry

    lax.fori_loop(0, blocks, invert, 0)
    width = heads * head
    kept[...] = jnp.zeros_like(kept)
    sent[...] = jnp.zeros_like(sent)
    total[...] = jnp.zeros_like(total)
    for copy in copies:
        copy.wait()
    queries = mine[:, :width] + theirs[:, :width]
    c, s = cosine[...], sine[...]
    for h in range(heads):
        v = queries[:, h * head:(h + 1) * head]
        q_ref[:, h * head:(h + 1) * head] = (v * c + swap_halves(v) * s).astype(BF16)
    a_ref[...] = (mine[:, width:] + theirs[:, width:]).astype(BF16)

    def destination(kb):
        spot = stored_at[jnp.maximum(kb, 0)]
        device = spot // 2
        away = jnp.where(device % 2 == own_core, 0, seq // 2)
        return pl.multiple_of(away + (device // 2) * (2 * BLOCK) + (spot % 2) * BLOCK, BLOCK)

    for j in range(rows // BLOCK):
        r0 = j * BLOCK
        block = order[0, own * (rows // BLOCK) + j]
        first = block - (span - 1)
        for w in range(span):
            source = pl.multiple_of(stored_at[jnp.maximum(first + w, 0)] * BLOCK, BLOCK)
            first_half, second_half = own_part[pl.ds(source, BLOCK), :], other_part[pl.ds(source, BLOCK), :]
            key_window[w * BLOCK:(w + 1) * BLOCK, :] = jnp.where(own_core == 0, first_half, second_half)
            value_window[w * BLOCK:(w + 1) * BLOCK, :] = jnp.where(own_core == 0, second_half, first_half)
        q = jnp.concatenate([q_ref[r0:r0 + BLOCK, h * head:(h + 1) * head] for h in range(heads)], 0)
        a = jnp.concatenate([a_ref[r0:r0 + BLOCK, h * head:(h + 1) * head] for h in range(heads)], 0)
        lane = lax.broadcasted_iota(jnp.int32, (1, heads * BLOCK), 1)
        query_place = block * BLOCK + lane % BLOCK
        start = jnp.zeros_like(query_place)
        end = jnp.int32(0)
        for d in range(lengths.shape[1]):
            end = end + lengths[0, d]
            start = jnp.where(query_place >= end, end, start)
        key_place = first * BLOCK + lax.broadcasted_iota(jnp.int32, (span * BLOCK, heads * BLOCK), 0)
        allowed = (key_place >= start) & (key_place <= query_place)
        k, v = key_window[...], value_window[...]
        scores = lax.dot_general(k, q, NT, preferred_element_type=F32) * scaling
        scores = jnp.where(allowed, scores, NEG)
        e = jnp.exp(scores - jnp.max(scores, axis=0, keepdims=True))
        weight = e * (1.0 / jnp.sum(e, axis=0, keepdims=True))
        probability = weight.astype(BF16)
        grad_probability = lax.dot_general(v, a, NT, preferred_element_type=F32)
        correction = jnp.sum(probability.astype(F32) * grad_probability, axis=0, keepdims=True)
        grad_score = (weight * (grad_probability - correction) * scaling).astype(BF16)
        key_part = lax.dot_general(grad_score, q, NN, preferred_element_type=F32)
        value_part = lax.dot_general(probability, a, NN, preferred_element_type=F32)
        for w in range(span):
            to = destination(first + w)
            total[pl.ds(to, BLOCK), :head] += key_part[w * BLOCK:(w + 1) * BLOCK]
            total[pl.ds(to, BLOCK), head:] += value_part[w * BLOCK:(w + 1) * BLOCK]
        g = lax.dot_general(k, grad_score, TN, preferred_element_type=F32).T
        for h in range(heads):
            u = g[h * BLOCK:(h + 1) * BLOCK]
            u = u * c[r0:r0 + BLOCK] - swap_halves(u) * s[r0:r0 + BLOCK]
            grad_query[r0:r0 + BLOCK, h * head:(h + 1) * head] = u.astype(BF16)
    half = seq // 2
    for j in range(rows // BLOCK):
        first = order[0, own * (rows // BLOCK) + j] - (span - 1)
        for w in range(span):
            spot = stored_at[jnp.maximum(first + w, 0)]
            device = spot // 2
            at = pl.multiple_of((device // 2) * (2 * BLOCK) + (spot % 2) * BLOCK, BLOCK)
            stays = device % 2 == own_core
            block = total[pl.ds(pl.multiple_of(jnp.where(stays, at, half + at), BLOCK), BLOCK), :].astype(BF16)

            @pl.when(stays)
            def _():
                kept[pl.ds(at, BLOCK), :] = block

            @pl.when(jnp.logical_not(stays))
            def _():
                sent[pl.ds(at, BLOCK), :] = block


def owner_kernel(pieces, cosine, sine, grad_key_value):
    head = cosine.shape[1]
    total = jnp.sum(pieces[...].astype(F32), axis=0)
    u = total[:, :head]
    grad_key_value[:, :head] = (u * cosine[...] - swap_halves(u) * sine[...]).astype(BF16)
    grad_key_value[:, head:] = total[:, head:].astype(BF16)


def weight_kernel(place, tokens, other_tokens, grads, other_grads, out):
    rows, features = tokens.shape
    core = place[0] % 2
    head = out.shape[2]
    both = jnp.concatenate([grads[:, head:], other_grads[:, head:]], axis=0)
    for chip in range(features // (2 * rows)):
        here = pl.ds(pl.multiple_of((2 * chip + core) * rows, rows), rows)
        t = jnp.concatenate([tokens[:, here], other_tokens[:, here]], axis=0)
        out[chip] = lax.dot_general(t, both, TN, preferred_element_type=F32).astype(BF16)


def input_kernel(place, grad_query, other_grad_query, grads, other_grads, own_weight, other_weight,
                 w0, w1, w2, w3, mine, theirs):
    rows, width = grad_query.shape
    head = own_weight.shape[1]
    core = place[0] % 2
    side = math.isqrt(own_weight.shape[0] // (2 * rows))
    queries = jnp.concatenate([grad_query[...], other_grad_query[...]], axis=0)
    both = jnp.concatenate([grads[...], other_grads[...]], axis=0)
    own_grad = jnp.where(core == 0, both[:, :head], both[:, head:])
    other_grad = jnp.where(core == 0, both[:, head:], both[:, :head])
    for n, shard in enumerate(shard_order(core, place[0] // 2, side)):
        at = (n % side) * rows
        here = pl.ds(pl.multiple_of(shard * rows, rows), rows)
        to = pl.ds(pl.multiple_of((shard // 2) * rows, rows), rows)
        part = (
            lax.dot_general(queries, (w0, w1, w2, w3)[n // side][at:at + rows, :width], NT,
                            preferred_element_type=F32)
            + lax.dot_general(own_grad, own_weight[here, :], NT, preferred_element_type=F32)
            + lax.dot_general(other_grad, other_weight[here, :], NT, preferred_element_type=F32)
        ).astype(BF16)
        mine[:, to] = part[:rows]
        theirs[:, to] = part[rows:]


def merge_kernel(place, mine, received, out):
    rows = out.shape[0]
    core = place[0] % 2
    for chip in range(mine.shape[1] // rows):
        for source, shard in ((mine, 2 * chip + core), (received, 2 * chip + 1 - core)):
            out[:, pl.ds(pl.multiple_of(shard * rows, rows), rows)] = source[:, chip * rows:(chip + 1) * rows]


def on_device(inputs, grad_output, query_weight, key_weight, value_weight, out_weight, doc_lengths, block_order):
    tokens, upstream = inputs[0], grad_output[0]
    rows, features = tokens.shape
    ctx, dp = lax.axis_size("ctx"), lax.axis_size("dp")
    chips = ctx // 2
    seq = rows * ctx
    me = lax.axis_index("ctx")
    core = me % 2
    head = key_weight.shape[1]
    width = query_weight.shape[1]
    heads = width // head
    planes = [[2 * i + c for i in range(chips)] for c in range(2)]
    other = [(i, i ^ 1) for i in range(ctx)]
    place = me.astype(jnp.int32).reshape(1)

    def to_chips(pieces):
        return lax.all_to_all(pieces, "ctx", 0, 0, tiled=True, axis_index_groups=planes)

    side = math.isqrt(chips)

    def moved(v, phase, step):
        pairs = []
        for row in range(side):
            for column in range(side):
                for c in range(2):
                    to = (row, (column + step) % side) if c == phase else ((row + step) % side, column)
                    pairs.append(((row * side + column) * 2 + c, (to[0] * side + to[1]) * 2 + c))
        return lax.ppermute(v, "ctx", pairs)

    rings = [[(row * side + i) * 2 for i in range(side)] for row in range(side)]
    rings += [[(i * side + column) * 2 + 1 for i in range(side)] for column in range(side)]
    (packed,) = call(pack_kernel, [shape((side, rows, 2 * width))], [HBM] * 2, (query_weight, out_weight), 0,
                     scratch=[pltpu.VMEM((rows, 2 * width), BF16), pltpu.VMEM((width, rows), BF16),
                              pltpu.SemaphoreType.DMA((2,)), pltpu.SemaphoreType.DMA((side,))],
                     limit=60, out_specs=[HBM])
    line = lax.all_to_all(packed, "ctx", 0, 0, tiled=True, axis_index_groups=rings).reshape(side * rows, 2 * width)
    held = [line] + [moved(line, 1, -offset) for offset in RING[1:]]

    chip_blocks = lax.dynamic_slice_in_dim(block_order[0], (me // 2) * 4, 4)
    chip_cosine, chip_sine = tables(chip_blocks, head)
    cosine = lax.dynamic_slice_in_dim(chip_cosine, core * rows, rows)
    sine = lax.dynamic_slice_in_dim(chip_sine, core * rows, rows)
    is_key = core == 0
    own_cosine = jnp.where(is_key, chip_cosine, 1.0)
    own_sine = jnp.where(is_key, chip_sine, 0.0)

    def swap(v):
        return lax.ppermute(v, "ctx", other)

    (copies,) = call(
        spread_kernel, [shape((chips, 2 * rows, head))], [SMEM] + [VMEM] * 3,
        (place, key_weight, value_weight, swap(jnp.where(is_key, value_weight, key_weight))), 0,
        scratch=[pltpu.VMEM((2 * rows, head), BF16), pltpu.SemaphoreType.DMA((chips,))], out_specs=[HBM])
    copies, _ = lax.optimization_barrier((copies, line))
    own_weight = to_chips(copies).reshape(features, head)
    other_tokens = swap(tokens)
    (projected,) = call(
        project_kernel, [shape((chips, 2 * rows, head))], [SMEM] + [VMEM] * 5,
        (place, tokens, other_tokens, own_weight, own_cosine, own_sine), 4 * rows * features * head,
        scratch=[pltpu.VMEM((2 * rows, head), BF16), pltpu.SemaphoreType.DMA((chips,))], out_specs=[HBM])
    sources = (place, tokens, upstream, other_tokens, swap(upstream))
    halves = [shape((rows, 2 * width), F32)] * 2
    mine, theirs = call(
        first_partial_kernel, halves, [SMEM] + [VMEM] * 7,
        sources + tuple(held[:3]), 3 * rows * features * width)
    mine, theirs = call(
        last_partial_kernel, halves, [SMEM] + [VMEM] * 7,
        sources + (held[3], mine, theirs), rows * features * width,
        scratch=[pltpu.VMEM((rows, 2 * width), F32), pltpu.SemaphoreType.DMA], out_specs=[VMEM, HBM])
    own_part = to_chips(projected).reshape(seq, head)
    own_part, mine, theirs = lax.optimization_barrier((own_part, mine, theirs))
    received = swap(theirs)
    other_part = swap(own_part)
    other_weight = swap(own_weight)
    window = LONGEST + 2 * BLOCK
    grad_query, kept, sent = call(
        attention_kernel,
        [shape((rows, width)), shape((seq // 2, 2 * head)), shape((seq // 2, 2 * head))],
        [SMEM] * 3 + [VMEM] + [HBM] * 3 + [VMEM] * 2,
        (place, block_order, doc_lengths, mine, received, own_part, other_part, cosine, sine),
        20 * rows * heads * window * head,
        scratch=[pltpu.VMEM((rows, width), BF16), pltpu.VMEM((rows, width), BF16),
                 pltpu.VMEM((window, head), BF16), pltpu.VMEM((window, head), BF16),
                 pltpu.VMEM((seq, 2 * head), F32), pltpu.SMEM((seq // BLOCK,), jnp.int32),
                 pltpu.VMEM((rows, 2 * width), F32),
                 pltpu.VMEM((seq, head), BF16), pltpu.VMEM((seq, head), BF16), pltpu.SemaphoreType.DMA((4,))],
        limit=28)
    pairs = (kept.astype(F32) + swap(sent).astype(F32)).astype(BF16)
    pieces, other_grad_query, other_weight = lax.optimization_barrier(
        (to_chips(pairs).reshape(chips, rows, 2 * head), swap(grad_query), other_weight))
    (grads,) = call(owner_kernel, [shape((rows, 2 * head))], [VMEM] * 3, (pieces, cosine, sine), 0)
    other_grads = swap(grads)
    (parts,) = call(
        weight_kernel, [shape((chips, rows, head))], [SMEM] + [VMEM] * 4,
        (place, tokens, other_tokens, grads, other_grads), 2 * rows * features * head)
    input_mine, input_theirs = call(
        input_kernel, [shape((rows, features // 2))] * 2, [SMEM] + [VMEM] * 10,
        (place, grad_query, other_grad_query, grads, other_grads, own_weight, other_weight, *held),
        2 * rows * features * (width + 2 * head))
    gathered, input_theirs = lax.optimization_barrier((to_chips(parts), input_theirs))
    grad_weight = jnp.sum(gathered.reshape(chips, rows, head).astype(F32), axis=0)
    group, step = dp, dp // 2
    while group > 4 and group % 2 == 0:
        sent_on = lax.ppermute(grad_weight.astype(BF16), "dp", [(i, i ^ step) for i in range(dp)])
        grad_weight = grad_weight.astype(BF16).astype(F32) + sent_on.astype(F32)
        group, step = group // 2, step // 2
    near = [[first + i for i in range(group)] for first in range(0, dp, group)]
    spread = jnp.broadcast_to(grad_weight.astype(BF16)[None], (group, rows, head))
    gathered = lax.all_to_all(spread, "dp", 0, 0, tiled=True, axis_index_groups=near)
    grad_weight = jnp.sum(gathered.reshape(group, rows, head).astype(F32), axis=0)
    (grad_input,) = call(
        merge_kernel, [shape((rows, features))], [SMEM] + [VMEM] * 2,
        (place, input_mine, swap(input_theirs)), 0)
    return grad_input[None], grad_weight


def solution(mesh):
    placed = (
        P("dp", "ctx", None),
        P("dp", "ctx", None),
        P("ctx", None),
        P("ctx", None),
        P("ctx", None),
        P(None, "ctx"),
        P("dp", None),
        P("dp", None),
    )
    return jax.shard_map(
        on_device,
        mesh=mesh,
        in_specs=placed,
        out_specs=(P("dp", "ctx", None), P("ctx", None)),
        check_vma=False,
    )
```

```python
import math

import jax
import jax.numpy as jnp
from jax import lax
from jax.experimental import pallas as pl
from jax.experimental.pallas import tpu as pltpu
from jax.sharding import PartitionSpec as P

THETA = 500000.0
NEG = -1e30
BLOCK = 64
LONGEST = 1024
RING = (0, 2, -1, 1)
BF16 = jnp.bfloat16
F32 = jnp.float32
NT = (((1,), (1,)), ((), ()))
TN = (((0,), (0,)), ((), ()))
NN = (((1,), (0,)), ((), ()))
VMEM = pl.BlockSpec(memory_space=pltpu.VMEM)
SMEM = pl.BlockSpec(memory_space=pltpu.SMEM)
HBM = pl.BlockSpec(memory_space=pltpu.HBM)


def call(body, outs, in_specs, args, flops, scratch=(), limit=24, out_specs=None):
    moved = sum(math.prod(a.shape) * a.dtype.itemsize for a in list(args) + list(outs))
    return pl.pallas_call(
        body,
        out_shape=outs,
        in_specs=in_specs,
        out_specs=out_specs or [VMEM] * len(outs),
        scratch_shapes=list(scratch),
        compiler_params=pltpu.CompilerParams(vmem_limit_bytes=limit << 20),
        cost_estimate=pl.CostEstimate(flops=flops, bytes_accessed=moved, transcendentals=0),
    )(*args)


def shape(dims, dtype=BF16):
    return jax.ShapeDtypeStruct(dims, dtype)


def tables(block_numbers, head_size):
    half = head_size // 2
    frequency = jnp.exp(-jnp.log(jnp.float32(THETA)) * (2.0 * jnp.arange(half, dtype=F32) / head_size))
    places = (block_numbers[:, None] * BLOCK + jnp.arange(BLOCK, dtype=jnp.int32)[None, :]).reshape(-1)
    phases = places.astype(F32)[:, None] * frequency[None, :]
    cosine, sine = jnp.cos(phases), jnp.sin(phases)
    return jnp.concatenate([cosine, cosine], 1), jnp.concatenate([-sine, sine], 1)


def swap_halves(v):
    return pltpu.roll(v, v.shape[-1] // 2, axis=1)


def fetch(sources, targets, arrived):
    copies = [pltpu.make_async_copy(a, b, arrived.at[i]) for i, (a, b) in enumerate(zip(sources, targets))]
    for copy in copies:
        copy.start()
    return copies


def write_copies(source, out, done):
    copies = [pltpu.make_async_copy(source, out.at[i], done.at[i]) for i in range(out.shape[0])]
    for copy in copies:
        copy.start()
    for copy in copies:
        copy.wait()


def pack_kernel(query_weight, out_weight, key_weight, value_weight, out, packed, turned, arrived, done):
    width, head = query_weight.shape[1], key_weight.shape[1]
    copies = fetch(
        (query_weight, out_weight, key_weight, value_weight),
        (packed.at[:, :width], turned, packed.at[:, 2 * width:2 * width + head], packed.at[:, 2 * width + head:]),
        arrived)
    copies[1].wait()
    packed[:, width:2 * width] = turned[...].T
    for copy in (copies[0], copies[2], copies[3]):
        copy.wait()
    write_copies(packed, out, done)


def split_kernel(line, big, small, copies, done):
    width = big.shape[1]
    small[...] = line[:, width:]
    started = [pltpu.make_async_copy(small, copies.at[i], done.at[i]) for i in range(copies.shape[0])]
    for copy in started:
        copy.start()
    big[...] = line[:, :width]
    for copy in started:
        copy.wait()


def shard_order(core, chip, side, natural=False):
    row, column = chip // side, chip % side
    order = []
    for second in range(side):
        for first in range(side):
            offset = RING[second]
            down = jnp.where(core == 0, second if natural else (row + offset + side) % side, first)
            along = jnp.where(core == 0, first, second if natural else (column + offset + side) % side)
            order.append((down * side + along) * 2 + core)
    return order


def partial_sums(place, sources, pieces, added, outs, begin, finished=None):
    rows, features = sources[0].shape
    width = outs[0].shape[1] // 2
    side = math.isqrt(features // (2 * rows))
    shards = shard_order(place[0] % 2, place[0] // 2, side)
    for which in (1, 0):
        for source, start in zip(sources[2 * which:], (0, width)):
            total = added[which][:, start:start + width] if begin else jnp.zeros((rows, width), F32)
            for n in range(0, side * len(pieces), 2):
                piece, at = pieces[n // side], (n % side) * rows
                columns = [pl.ds(pl.multiple_of(shards[begin * side + n + i] * rows, rows), rows) for i in range(2)]
                t = jnp.concatenate([source[:, here] for here in columns], axis=1)
                total += lax.dot_general(t, piece[at:at + 2 * rows, start:start + width], NN,
                                         preferred_element_type=F32)
            outs[which][:, start:start + width] = total
        if which and finished:
            finished()


def first_partial_kernel(place, tokens, upstream, other_tokens, other_upstream, w0, w1, w2, mine, theirs):
    partial_sums(place, (tokens, upstream, other_tokens, other_upstream), (w0, w1, w2), None, (mine, theirs), 0)


def last_partial_kernel(place, tokens, upstream, other_tokens, other_upstream, w3, mine_before, theirs_before,
                        mine, theirs_out, theirs, done):
    copy = pltpu.make_async_copy(theirs, theirs_out, done)
    partial_sums(place, (tokens, upstream, other_tokens, other_upstream), (w3,), (mine_before, theirs_before),
                 (mine, theirs), 3, copy.start)
    copy.wait()


def project_kernel(place, tokens, other_tokens, weights, mine, theirs):
    rows, features = tokens.shape
    side = math.isqrt(features // (2 * rows))
    shards = shard_order(place[0] % 2, place[0] // 2, side, natural=True)
    for source, out in ((other_tokens, theirs), (tokens, mine)):
        total = jnp.zeros(out.shape, F32)
        for n in range(0, side * side, 2):
            columns = [pl.ds(pl.multiple_of(shards[n + i] * rows, rows), rows) for i in range(2)]
            t = jnp.concatenate([source[:, here] for here in columns], axis=1)
            total += lax.dot_general(t, weights[n * rows:(n + 2) * rows, :], NN, preferred_element_type=F32)
        out[...] = total


def rotate_kernel(mine, received, cosine, sine, out):
    head = cosine.shape[1]
    both = mine[...] + received[...]
    key = both[:, :head]
    key = (key * cosine[...] + swap_halves(key) * sine[...]).astype(BF16)
    value = both[:, head:].astype(BF16)
    for chip in range(out.shape[0]):
        out[chip, :, :head] = key
        out[chip, :, head:] = value


def attention_kernel(place, order, lengths, mine, theirs_at, own_at, other_at, cosine, sine,
                     grad_query, kept, sent, q_ref, a_ref, key_window, value_window, total, stored_at,
                     theirs, own_part, other_part, arrived):
    copies = fetch((theirs_at, own_at, other_at), (theirs, own_part, other_part), arrived)
    rows = mine.shape[0]
    head = cosine.shape[1]
    heads = q_ref.shape[1] // head
    seq = 2 * own_part.shape[0]
    blocks = seq // BLOCK
    span = key_window.shape[0] // BLOCK
    scaling = head ** (-0.5)
    own = place[0]
    own_core = own % 2

    def invert(i, carry):
        stored_at[order[0, i]] = i
        return carry

    lax.fori_loop(0, blocks, invert, 0)
    width = heads * head
    kept[...] = jnp.zeros_like(kept)
    sent[...] = jnp.zeros_like(sent)
    total[...] = jnp.zeros_like(total)
    for copy in copies:
        copy.wait()
    queries = mine[:, :width] + theirs[:, :width]
    c, s = cosine[...], sine[...]
    for h in range(heads):
        v = queries[:, h * head:(h + 1) * head]
        q_ref[:, h * head:(h + 1) * head] = (v * c + swap_halves(v) * s).astype(BF16)
    a_ref[...] = (mine[:, width:] + theirs[:, width:]).astype(BF16)

    def destination(kb):
        spot = stored_at[jnp.maximum(kb, 0)]
        device = spot // 2
        away = jnp.where(device % 2 == own_core, 0, seq // 2)
        return pl.multiple_of(away + (device // 2) * (2 * BLOCK) + (spot % 2) * BLOCK, BLOCK)

    for j in range(rows // BLOCK):
        r0 = j * BLOCK
        block = order[0, own * (rows // BLOCK) + j]
        first = block - (span - 1)
        for w in range(span):
            spot = stored_at[jnp.maximum(first + w, 0)]
            device = spot // 2
            source = pl.multiple_of((device // 2) * (2 * BLOCK) + (spot % 2) * BLOCK, BLOCK)
            block_here = jnp.where(
                device % 2 == own_core, own_part[pl.ds(source, BLOCK), :], other_part[pl.ds(source, BLOCK), :])
            key_window[w * BLOCK:(w + 1) * BLOCK, :] = block_here[:, :head]
            value_window[w * BLOCK:(w + 1) * BLOCK, :] = block_here[:, head:]
        q = jnp.concatenate([q_ref[r0:r0 + BLOCK, h * head:(h + 1) * head] for h in range(heads)], 0)
        a = jnp.concatenate([a_ref[r0:r0 + BLOCK, h * head:(h + 1) * head] for h in range(heads)], 0)
        lane = lax.broadcasted_iota(jnp.int32, (1, heads * BLOCK), 1)
        query_place = block * BLOCK + lane % BLOCK
        start = jnp.zeros_like(query_place)
        end = jnp.int32(0)
        for d in range(lengths.shape[1]):
            end = end + lengths[0, d]
            start = jnp.where(query_place >= end, end, start)
        key_place = first * BLOCK + lax.broadcasted_iota(jnp.int32, (span * BLOCK, heads * BLOCK), 0)
        allowed = (key_place >= start) & (key_place <= query_place)
        k, v = key_window[...], value_window[...]
        scores = lax.dot_general(k, q, NT, preferred_element_type=F32) * scaling
        scores = jnp.where(allowed, scores, NEG)
        e = jnp.exp(scores - jnp.max(scores, axis=0, keepdims=True))
        weight = e * (1.0 / jnp.sum(e, axis=0, keepdims=True))
        probability = weight.astype(BF16)
        grad_probability = lax.dot_general(v, a, NT, preferred_element_type=F32)
        correction = jnp.sum(probability.astype(F32) * grad_probability, axis=0, keepdims=True)
        grad_score = (weight * (grad_probability - correction) * scaling).astype(BF16)
        key_part = lax.dot_general(grad_score, q, NN, preferred_element_type=F32)
        value_part = lax.dot_general(probability, a, NN, preferred_element_type=F32)
        for w in range(span):
            to = destination(first + w)
            total[pl.ds(to, BLOCK), :head] += key_part[w * BLOCK:(w + 1) * BLOCK]
            total[pl.ds(to, BLOCK), head:] += value_part[w * BLOCK:(w + 1) * BLOCK]
        g = lax.dot_general(k, grad_score, TN, preferred_element_type=F32).T
        for h in range(heads):
            u = g[h * BLOCK:(h + 1) * BLOCK]
            u = u * c[r0:r0 + BLOCK] - swap_halves(u) * s[r0:r0 + BLOCK]
            grad_query[r0:r0 + BLOCK, h * head:(h + 1) * head] = u.astype(BF16)
    half = seq // 2
    for j in range(rows // BLOCK):
        first = order[0, own * (rows // BLOCK) + j] - (span - 1)
        for w in range(span):
            spot = stored_at[jnp.maximum(first + w, 0)]
            device = spot // 2
            at = pl.multiple_of((device // 2) * (2 * BLOCK) + (spot % 2) * BLOCK, BLOCK)
            stays = device % 2 == own_core
            block = total[pl.ds(pl.multiple_of(jnp.where(stays, at, half + at), BLOCK), BLOCK), :].astype(BF16)

            @pl.when(stays)
            def _():
                kept[pl.ds(at, BLOCK), :] = block

            @pl.when(jnp.logical_not(stays))
            def _():
                sent[pl.ds(at, BLOCK), :] = block


def owner_kernel(pieces, cosine, sine, grad_key_value):
    head = cosine.shape[1]
    total = jnp.sum(pieces[...].astype(F32), axis=0)
    u = total[:, :head]
    grad_key_value[:, :head] = (u * cosine[...] - swap_halves(u) * sine[...]).astype(BF16)
    grad_key_value[:, head:] = total[:, head:].astype(BF16)


def weight_kernel(place, tokens, other_tokens, grads, other_grads, out):
    rows, features = tokens.shape
    core = place[0] % 2
    head = out.shape[2]
    both = jnp.concatenate([grads[:, head:], other_grads[:, head:]], axis=0)
    for chip in range(features // (2 * rows)):
        here = pl.ds(pl.multiple_of((2 * chip + core) * rows, rows), rows)
        t = jnp.concatenate([tokens[:, here], other_tokens[:, here]], axis=0)
        out[chip] = lax.dot_general(t, both, TN, preferred_element_type=F32).astype(BF16)


def input_kernel(place, grad_query, other_grad_query, grads, other_grads, weights, w0, w1, w2, w3, mine, theirs):
    rows, width = grad_query.shape
    core, chip = place[0] % 2, place[0] // 2
    side = math.isqrt(weights.shape[0] // rows)
    queries = jnp.concatenate([grad_query[...], other_grad_query[...]], axis=0)
    both = jnp.concatenate([grads[...], other_grads[...]], axis=0)
    own_place = jnp.where(core == 0, chip // side, chip % side)
    for n, shard in enumerate(shard_order(core, chip, side)):
        at = (n % side) * rows
        held_at = ((own_place + RING[n // side] + side) % side) * side + n % side
        small = weights[pl.ds(pl.multiple_of(held_at * rows, rows), rows), :]
        to = pl.ds(pl.multiple_of((shard // 2) * rows, rows), rows)
        part = (
            lax.dot_general(queries, (w0, w1, w2, w3)[n // side][at:at + rows, :width], NT,
                            preferred_element_type=F32)
            + lax.dot_general(both, small, NT, preferred_element_type=F32)
        ).astype(BF16)
        mine[:, to] = part[:rows]
        theirs[:, to] = part[rows:]


def merge_kernel(place, mine, received, out):
    rows = out.shape[0]
    core = place[0] % 2
    for chip in range(mine.shape[1] // rows):
        for source, shard in ((mine, 2 * chip + core), (received, 2 * chip + 1 - core)):
            out[:, pl.ds(pl.multiple_of(shard * rows, rows), rows)] = source[:, chip * rows:(chip + 1) * rows]


def on_device(inputs, grad_output, query_weight, key_weight, value_weight, out_weight, doc_lengths, block_order):
    tokens, upstream = inputs[0], grad_output[0]
    rows, features = tokens.shape
    ctx, dp = lax.axis_size("ctx"), lax.axis_size("dp")
    chips = ctx // 2
    seq = rows * ctx
    me = lax.axis_index("ctx")
    head = key_weight.shape[1]
    width = query_weight.shape[1]
    heads = width // head
    planes = [[2 * i + c for i in range(chips)] for c in range(2)]
    other = [(i, i ^ 1) for i in range(ctx)]
    place = me.astype(jnp.int32).reshape(1)

    def to_chips(pieces):
        return lax.all_to_all(pieces, "ctx", 0, 0, tiled=True, axis_index_groups=planes)

    side = math.isqrt(chips)

    def moved(v, phase, step):
        pairs = []
        for row in range(side):
            for column in range(side):
                for c in range(2):
                    to = (row, (column + step) % side) if c == phase else ((row + step) % side, column)
                    pairs.append(((row * side + column) * 2 + c, (to[0] * side + to[1]) * 2 + c))
        return lax.ppermute(v, "ctx", pairs)

    rings = [[(row * side + i) * 2 for i in range(side)] for row in range(side)]
    rings += [[(i * side + column) * 2 + 1 for i in range(side)] for column in range(side)]
    crossing = [[(i * side + column) * 2 for i in range(side)] for column in range(side)]
    crossing += [[(row * side + i) * 2 + 1 for i in range(side)] for row in range(side)]
    (packed,) = call(
        pack_kernel, [shape((side, rows, 2 * width + 2 * head))], [HBM] * 4,
        (query_weight, out_weight, key_weight, value_weight), 0,
        scratch=[pltpu.VMEM((rows, 2 * width + 2 * head), BF16), pltpu.VMEM((width, rows), BF16),
                 pltpu.SemaphoreType.DMA((4,)), pltpu.SemaphoreType.DMA((side,))],
        limit=60, out_specs=[HBM])
    line = lax.all_to_all(packed, "ctx", 0, 0, tiled=True, axis_index_groups=rings)
    line = line.reshape(side * rows, 2 * width + 2 * head)
    line, small, copies = call(
        split_kernel,
        [shape((side * rows, 2 * width)), shape((side * rows, 2 * head)), shape((side, side * rows, 2 * head))],
        [VMEM], (line,), 0, scratch=[pltpu.SemaphoreType.DMA((side,))], out_specs=[VMEM, VMEM, HBM])
    small_weights = lax.all_to_all(
        copies, "ctx", 0, 0, tiled=True, axis_index_groups=crossing).reshape(features // 2, 2 * head)
    held = [line] + [moved(line, 1, -offset) for offset in RING[1:]]

    cosine, sine = tables(lax.dynamic_slice_in_dim(block_order[0], me * 2, 2), head)

    def swap(v):
        return lax.ppermute(v, "ctx", other)

    other_tokens = swap(tokens)
    kv_mine, kv_theirs = call(
        project_kernel, [shape((rows, 2 * head), F32)] * 2, [SMEM] + [VMEM] * 3,
        (place, tokens, other_tokens, small_weights), 4 * rows * features * head)
    (projected,) = call(
        rotate_kernel, [shape((chips, rows, 2 * head))], [VMEM] * 4, (kv_mine, swap(kv_theirs), cosine, sine), 0)
    sources = (place, tokens, upstream, other_tokens, swap(upstream))
    halves = [shape((rows, 2 * width), F32)] * 2
    mine, theirs = call(
        first_partial_kernel, halves, [SMEM] + [VMEM] * 7,
        sources + tuple(held[:3]), 3 * rows * features * width)
    mine, theirs = call(
        last_partial_kernel, halves, [SMEM] + [VMEM] * 7,
        sources + (held[3], mine, theirs), rows * features * width,
        scratch=[pltpu.VMEM((rows, 2 * width), F32), pltpu.SemaphoreType.DMA], out_specs=[VMEM, HBM])
    own_part = to_chips(projected).reshape(seq // 2, 2 * head)
    own_part, theirs = lax.optimization_barrier((own_part, theirs))
    received = swap(theirs)
    other_part = swap(own_part)
    window = LONGEST + BLOCK
    grad_query, kept, sent = call(
        attention_kernel,
        [shape((rows, width)), shape((seq // 2, 2 * head)), shape((seq // 2, 2 * head))],
        [SMEM] * 3 + [VMEM] + [HBM] * 3 + [VMEM] * 2,
        (place, block_order, doc_lengths, mine, received, own_part, other_part, cosine, sine),
        20 * rows * heads * window * head,
        scratch=[pltpu.VMEM((rows, width), BF16), pltpu.VMEM((rows, width), BF16),
                 pltpu.VMEM((window, head), BF16), pltpu.VMEM((window, head), BF16),
                 pltpu.VMEM((seq, 2 * head), F32), pltpu.SMEM((seq // BLOCK,), jnp.int32),
                 pltpu.VMEM((rows, 2 * width), F32),
                 pltpu.VMEM((seq // 2, 2 * head), BF16), pltpu.VMEM((seq // 2, 2 * head), BF16),
                 pltpu.SemaphoreType.DMA((4,))],
        limit=28)
    pairs = (kept.astype(F32) + swap(sent).astype(F32)).astype(BF16)
    pieces, other_grad_query = lax.optimization_barrier(
        (to_chips(pairs).reshape(chips, rows, 2 * head), swap(grad_query)))
    (grads,) = call(owner_kernel, [shape((rows, 2 * head))], [VMEM] * 3, (pieces, cosine, sine), 0)
    other_grads = swap(grads)
    (parts,) = call(
        weight_kernel, [shape((chips, rows, head))], [SMEM] + [VMEM] * 4,
        (place, tokens, other_tokens, grads, other_grads), 2 * rows * features * head)
    input_mine, input_theirs = call(
        input_kernel, [shape((rows, features // 2))] * 2, [SMEM] + [VMEM] * 9,
        (place, grad_query, other_grad_query, grads, other_grads, small_weights, *held),
        2 * rows * features * (width + 2 * head))
    gathered, input_theirs = lax.optimization_barrier((to_chips(parts), input_theirs))
    grad_weight = jnp.sum(gathered.reshape(chips, rows, head).astype(F32), axis=0)
    group, step = dp, dp // 2
    while group > 4 and group % 2 == 0:
        sent_on = lax.ppermute(grad_weight.astype(BF16), "dp", [(i, i ^ step) for i in range(dp)])
        grad_weight = grad_weight.astype(BF16).astype(F32) + sent_on.astype(F32)
        group, step = group // 2, step // 2
    near = [[first + i for i in range(group)] for first in range(0, dp, group)]
    spread = jnp.broadcast_to(grad_weight.astype(BF16)[None], (group, rows, head))
    gathered = lax.all_to_all(spread, "dp", 0, 0, tiled=True, axis_index_groups=near)
    (grad_input,) = call(
        merge_kernel, [shape((rows, features))], [SMEM] + [VMEM] * 2,
        (place, input_mine, swap(input_theirs)), 0)
    gathered, grad_input = lax.optimization_barrier((gathered, grad_input))
    grad_weight = jnp.sum(gathered.reshape(group, rows, head).astype(F32), axis=0)
    return grad_input[None], grad_weight


def solution(mesh):
    placed = (
        P("dp", "ctx", None),
        P("dp", "ctx", None),
        P("ctx", None),
        P("ctx", None),
        P("ctx", None),
        P(None, "ctx"),
        P("dp", None),
        P("dp", None),
    )
    return jax.shard_map(
        on_device,
        mesh=mesh,
        in_specs=placed,
        out_specs=(P("dp", "ctx", None), P("ctx", None)),
        check_vma=False,
    )
```

```python
import math

import jax
import jax.numpy as jnp
from jax import lax
from jax.experimental import pallas as pl
from jax.experimental.pallas import tpu as pltpu
from jax.sharding import PartitionSpec as P

THETA = 500000.0
NEG = -1e30
BLOCK = 64
LONGEST = 1024
RING = (0, 2, -1, 1)
BF16 = jnp.bfloat16
F32 = jnp.float32
NT = (((1,), (1,)), ((), ()))
TN = (((0,), (0,)), ((), ()))
NN = (((1,), (0,)), ((), ()))
VMEM = pl.BlockSpec(memory_space=pltpu.VMEM)
SMEM = pl.BlockSpec(memory_space=pltpu.SMEM)
HBM = pl.BlockSpec(memory_space=pltpu.HBM)


def call(body, outs, in_specs, args, flops, scratch=(), limit=24, out_specs=None):
    moved = sum(math.prod(a.shape) * a.dtype.itemsize for a in list(args) + list(outs))
    return pl.pallas_call(
        body,
        out_shape=outs,
        in_specs=in_specs,
        out_specs=out_specs or [VMEM] * len(outs),
        scratch_shapes=list(scratch),
        compiler_params=pltpu.CompilerParams(vmem_limit_bytes=limit << 20),
        cost_estimate=pl.CostEstimate(flops=flops, bytes_accessed=moved, transcendentals=0),
    )(*args)


def shape(dims, dtype=BF16):
    return jax.ShapeDtypeStruct(dims, dtype)


def tables(block_numbers, head_size):
    half = head_size // 2
    frequency = jnp.exp(-jnp.log(jnp.float32(THETA)) * (2.0 * jnp.arange(half, dtype=F32) / head_size))
    places = (block_numbers[:, None] * BLOCK + jnp.arange(BLOCK, dtype=jnp.int32)[None, :]).reshape(-1)
    phases = places.astype(F32)[:, None] * frequency[None, :]
    cosine, sine = jnp.cos(phases), jnp.sin(phases)
    return jnp.concatenate([cosine, cosine], 1), jnp.concatenate([-sine, sine], 1)


def swap_halves(v):
    return pltpu.roll(v, v.shape[-1] // 2, axis=1)


def fetch(sources, targets, arrived):
    copies = [pltpu.make_async_copy(a, b, arrived.at[i]) for i, (a, b) in enumerate(zip(sources, targets))]
    for copy in copies:
        copy.start()
    return copies


def write_copies(source, out, done):
    copies = [pltpu.make_async_copy(source, out.at[i], done.at[i]) for i in range(out.shape[0])]
    for copy in copies:
        copy.start()
    for copy in copies:
        copy.wait()


def pack_kernel(query_weight, out_weight, key_weight, value_weight, out, packed, turned, arrived, done):
    width, head = query_weight.shape[1], key_weight.shape[1]
    copies = fetch(
        (query_weight, out_weight, key_weight, value_weight),
        (packed.at[:, :width], turned, packed.at[:, 2 * width:2 * width + head], packed.at[:, 2 * width + head:]),
        arrived)
    copies[1].wait()
    packed[:, width:2 * width] = turned[...].T
    for copy in (copies[0], copies[2], copies[3]):
        copy.wait()
    write_copies(packed, out, done)


def split_kernel(line, big, small, copies, done):
    width = big.shape[1]
    small[...] = line[:, width:]
    started = [pltpu.make_async_copy(small, copies.at[i], done.at[i]) for i in range(copies.shape[0])]
    for copy in started:
        copy.start()
    big[...] = line[:, :width]
    for copy in started:
        copy.wait()


def shard_order(core, chip, side, natural=False):
    row, column = chip // side, chip % side
    order = []
    for second in range(side):
        for first in range(side):
            offset = RING[second]
            down = jnp.where(core == 0, second if natural else (row + offset + side) % side, first)
            along = jnp.where(core == 0, first, second if natural else (column + offset + side) % side)
            order.append((down * side + along) * 2 + core)
    return order


def partial_sums(place, sources, pieces, added, outs, begin, finished=None):
    rows, features = sources[0].shape
    width = outs[0].shape[1] // 2
    side = math.isqrt(features // (2 * rows))
    shards = shard_order(place[0] % 2, place[0] // 2, side)
    for which in (1, 0):
        for source, start in zip(sources[2 * which:], (0, width)):
            total = added[which][:, start:start + width] if begin else jnp.zeros((rows, width), F32)
            for n in range(0, side * len(pieces), 2):
                piece, at = pieces[n // side], (n % side) * rows
                columns = [pl.ds(pl.multiple_of(shards[begin * side + n + i] * rows, rows), rows) for i in range(2)]
                t = jnp.concatenate([source[:, here] for here in columns], axis=1)
                total += lax.dot_general(t, piece[at:at + 2 * rows, start:start + width], NN,
                                         preferred_element_type=F32)
            outs[which][:, start:start + width] = total
        if which and finished:
            finished()


def first_partial_kernel(place, tokens, upstream, other_tokens, other_upstream, w0, w1, w2, mine, theirs):
    partial_sums(place, (tokens, upstream, other_tokens, other_upstream), (w0, w1, w2), None, (mine, theirs), 0)


def last_partial_kernel(place, tokens, upstream, other_tokens, other_upstream, w3, mine_before, theirs_before,
                        mine, theirs_out, theirs, done):
    copy = pltpu.make_async_copy(theirs, theirs_out, done)
    partial_sums(place, (tokens, upstream, other_tokens, other_upstream), (w3,), (mine_before, theirs_before),
                 (mine, theirs), 3, copy.start)
    copy.wait()


def project_kernel(place, tokens, other_tokens, weights, mine, theirs):
    rows, features = tokens.shape
    side = math.isqrt(features // (2 * rows))
    shards = shard_order(place[0] % 2, place[0] // 2, side, natural=True)
    for source, out in ((other_tokens, theirs), (tokens, mine)):
        total = jnp.zeros(out.shape, F32)
        for n in range(0, side * side, 2):
            columns = [pl.ds(pl.multiple_of(shards[n + i] * rows, rows), rows) for i in range(2)]
            t = jnp.concatenate([source[:, here] for here in columns], axis=1)
            total += lax.dot_general(t, weights[n * rows:(n + 2) * rows, :], NN, preferred_element_type=F32)
        out[...] = total


def rotate_kernel(mine, received, cosine, sine, out):
    head = cosine.shape[1]
    both = mine[...] + received[...]
    key = both[:, :head]
    key = (key * cosine[...] + swap_halves(key) * sine[...]).astype(BF16)
    value = both[:, head:].astype(BF16)
    for chip in range(out.shape[0]):
        out[chip, :, :head] = key
        out[chip, :, head:] = value


def attention_kernel(place, order, lengths, mine, theirs_at, own_at, other_at, cosine, sine,
                     grad_query, kept, sent, q_ref, a_ref, key_window, value_window, total, stored_at,
                     theirs, own_part, other_part, arrived):
    copies = fetch((theirs_at, own_at, other_at), (theirs, own_part, other_part), arrived)
    rows = mine.shape[0]
    head = cosine.shape[1]
    heads = q_ref.shape[1] // head
    seq = 2 * own_part.shape[0]
    blocks = seq // BLOCK
    span = key_window.shape[0] // BLOCK
    scaling = head ** (-0.5)
    own = place[0]
    own_core = own % 2

    def invert(i, carry):
        stored_at[order[0, i]] = i
        return carry

    lax.fori_loop(0, blocks, invert, 0)
    width = heads * head
    kept[...] = jnp.zeros_like(kept)
    sent[...] = jnp.zeros_like(sent)
    total[...] = jnp.zeros_like(total)
    for copy in copies:
        copy.wait()
    queries = mine[:, :width] + theirs[:, :width]
    c, s = cosine[...], sine[...]
    for h in range(heads):
        v = queries[:, h * head:(h + 1) * head]
        q_ref[:, h * head:(h + 1) * head] = (v * c + swap_halves(v) * s).astype(BF16)
    a_ref[...] = (mine[:, width:] + theirs[:, width:]).astype(BF16)

    def destination(kb):
        spot = stored_at[jnp.maximum(kb, 0)]
        device = spot // 2
        away = jnp.where(device % 2 == own_core, 0, seq // 2)
        return pl.multiple_of(away + (device // 2) * (2 * BLOCK) + (spot % 2) * BLOCK, BLOCK)

    for j in range(rows // BLOCK):
        r0 = j * BLOCK
        block = order[0, own * (rows // BLOCK) + j]
        first = block - (span - 1)
        for w in range(span):
            spot = stored_at[jnp.maximum(first + w, 0)]
            device = spot // 2
            source = pl.multiple_of((device // 2) * (2 * BLOCK) + (spot % 2) * BLOCK, BLOCK)
            block_here = jnp.where(
                device % 2 == own_core, own_part[pl.ds(source, BLOCK), :], other_part[pl.ds(source, BLOCK), :])
            key_window[w * BLOCK:(w + 1) * BLOCK, :] = block_here[:, :head]
            value_window[w * BLOCK:(w + 1) * BLOCK, :] = block_here[:, head:]
        q = jnp.concatenate([q_ref[r0:r0 + BLOCK, h * head:(h + 1) * head] for h in range(heads)], 0)
        a = jnp.concatenate([a_ref[r0:r0 + BLOCK, h * head:(h + 1) * head] for h in range(heads)], 0)
        lane = lax.broadcasted_iota(jnp.int32, (1, heads * BLOCK), 1)
        query_place = block * BLOCK + lane % BLOCK
        start = jnp.zeros_like(query_place)
        end = jnp.int32(0)
        for d in range(lengths.shape[1]):
            end = end + lengths[0, d]
            start = jnp.where(query_place >= end, end, start)
        key_place = first * BLOCK + lax.broadcasted_iota(jnp.int32, (span * BLOCK, heads * BLOCK), 0)
        allowed = (key_place >= start) & (key_place <= query_place)
        k, v = key_window[...], value_window[...]
        scores = lax.dot_general(k, q, NT, preferred_element_type=F32) * scaling
        scores = jnp.where(allowed, scores, NEG)
        e = jnp.exp(scores - jnp.max(scores, axis=0, keepdims=True))
        weight = e * (1.0 / jnp.sum(e, axis=0, keepdims=True))
        probability = weight.astype(BF16)
        grad_probability = lax.dot_general(v, a, NT, preferred_element_type=F32)
        correction = jnp.sum(probability.astype(F32) * grad_probability, axis=0, keepdims=True)
        grad_score = (weight * (grad_probability - correction) * scaling).astype(BF16)
        key_part = lax.dot_general(grad_score, q, NN, preferred_element_type=F32)
        value_part = lax.dot_general(probability, a, NN, preferred_element_type=F32)
        for w in range(span):
            to = destination(first + w)
            total[pl.ds(to, BLOCK), :head] += key_part[w * BLOCK:(w + 1) * BLOCK]
            total[pl.ds(to, BLOCK), head:] += value_part[w * BLOCK:(w + 1) * BLOCK]
        g = lax.dot_general(k, grad_score, TN, preferred_element_type=F32).T
        for h in range(heads):
            u = g[h * BLOCK:(h + 1) * BLOCK]
            u = u * c[r0:r0 + BLOCK] - swap_halves(u) * s[r0:r0 + BLOCK]
            grad_query[r0:r0 + BLOCK, h * head:(h + 1) * head] = u.astype(BF16)
    half = seq // 2
    for j in range(rows // BLOCK):
        first = order[0, own * (rows // BLOCK) + j] - (span - 1)
        for w in range(span):
            spot = stored_at[jnp.maximum(first + w, 0)]
            device = spot // 2
            at = pl.multiple_of((device // 2) * (2 * BLOCK) + (spot % 2) * BLOCK, BLOCK)
            stays = device % 2 == own_core
            block = total[pl.ds(pl.multiple_of(jnp.where(stays, at, half + at), BLOCK), BLOCK), :].astype(BF16)

            @pl.when(stays)
            def _():
                kept[pl.ds(at, BLOCK), :] = block

            @pl.when(jnp.logical_not(stays))
            def _():
                sent[pl.ds(at, BLOCK), :] = block


def owner_kernel(pieces, cosine, sine, grad_key_value):
    head = cosine.shape[1]
    total = jnp.sum(pieces[...].astype(F32), axis=0)
    u = total[:, :head]
    grad_key_value[:, :head] = (u * cosine[...] - swap_halves(u) * sine[...]).astype(BF16)
    grad_key_value[:, head:] = total[:, head:].astype(BF16)


def weight_kernel(place, tokens, other_tokens, grads, other_grads, out):
    rows, features = tokens.shape
    core = place[0] % 2
    head = out.shape[2]
    both = jnp.concatenate([grads[:, head:], other_grads[:, head:]], axis=0)
    for chip in range(features // (2 * rows)):
        here = pl.ds(pl.multiple_of((2 * chip + core) * rows, rows), rows)
        t = jnp.concatenate([tokens[:, here], other_tokens[:, here]], axis=0)
        out[chip] = lax.dot_general(t, both, TN, preferred_element_type=F32).astype(BF16)


def input_kernel(place, grad_query, other_grad_query, grads, other_grads, weights, w0, w1, w2, w3, mine, theirs):
    rows, width = grad_query.shape
    core, chip = place[0] % 2, place[0] // 2
    side = math.isqrt(weights.shape[0] // rows)
    queries = jnp.concatenate([grad_query[...], other_grad_query[...]], axis=0)
    both = jnp.concatenate([grads[...], other_grads[...]], axis=0)
    own_place = jnp.where(core == 0, chip // side, chip % side)
    for n, shard in enumerate(shard_order(core, chip, side)):
        at = (n % side) * rows
        held_at = ((own_place + RING[n // side] + side) % side) * side + n % side
        small = weights[pl.ds(pl.multiple_of(held_at * rows, rows), rows), :]
        to = pl.ds(pl.multiple_of((shard // 2) * rows, rows), rows)
        part = (
            lax.dot_general(queries, (w0, w1, w2, w3)[n // side][at:at + rows, :width], NT,
                            preferred_element_type=F32)
            + lax.dot_general(both, small, NT, preferred_element_type=F32)
        ).astype(BF16)
        mine[:, to] = part[:rows]
        theirs[:, to] = part[rows:]


def merge_kernel(place, mine, received, out):
    rows = out.shape[0]
    core = place[0] % 2
    for chip in range(mine.shape[1] // rows):
        for source, shard in ((mine, 2 * chip + core), (received, 2 * chip + 1 - core)):
            out[:, pl.ds(pl.multiple_of(shard * rows, rows), rows)] = source[:, chip * rows:(chip + 1) * rows]


def on_device(inputs, grad_output, query_weight, key_weight, value_weight, out_weight, doc_lengths, block_order):
    tokens, upstream = inputs[0], grad_output[0]
    rows, features = tokens.shape
    ctx, dp = lax.axis_size("ctx"), lax.axis_size("dp")
    chips = ctx // 2
    seq = rows * ctx
    me = lax.axis_index("ctx")
    head = key_weight.shape[1]
    width = query_weight.shape[1]
    heads = width // head
    planes = [[2 * i + c for i in range(chips)] for c in range(2)]
    other = [(i, i ^ 1) for i in range(ctx)]
    place = me.astype(jnp.int32).reshape(1)

    def to_chips(pieces):
        return lax.all_to_all(pieces, "ctx", 0, 0, tiled=True, axis_index_groups=planes)

    side = math.isqrt(chips)

    def moved(v, phase, step):
        pairs = []
        for row in range(side):
            for column in range(side):
                for c in range(2):
                    to = (row, (column + step) % side) if c == phase else ((row + step) % side, column)
                    pairs.append(((row * side + column) * 2 + c, (to[0] * side + to[1]) * 2 + c))
        return lax.ppermute(v, "ctx", pairs)

    rings = [[(row * side + i) * 2 for i in range(side)] for row in range(side)]
    rings += [[(i * side + column) * 2 + 1 for i in range(side)] for column in range(side)]
    crossing = [[(i * side + column) * 2 for i in range(side)] for column in range(side)]
    crossing += [[(row * side + i) * 2 + 1 for i in range(side)] for row in range(side)]
    (packed,) = call(
        pack_kernel, [shape((side, rows, 2 * width + 2 * head))], [HBM] * 4,
        (query_weight, out_weight, key_weight, value_weight), 0,
        scratch=[pltpu.VMEM((rows, 2 * width + 2 * head), BF16), pltpu.VMEM((width, rows), BF16),
                 pltpu.SemaphoreType.DMA((4,)), pltpu.SemaphoreType.DMA((side,))],
        limit=60, out_specs=[HBM])
    line = lax.all_to_all(packed, "ctx", 0, 0, tiled=True, axis_index_groups=rings)
    line = line.reshape(side * rows, 2 * width + 2 * head)
    line, small, copies = call(
        split_kernel,
        [shape((side * rows, 2 * width)), shape((side * rows, 2 * head)), shape((side, side * rows, 2 * head))],
        [VMEM], (line,), 0, scratch=[pltpu.SemaphoreType.DMA((side,))], out_specs=[VMEM, VMEM, HBM])
    small_weights = lax.all_to_all(
        copies, "ctx", 0, 0, tiled=True, axis_index_groups=crossing).reshape(features // 2, 2 * head)
    held = [line] + [moved(line, 1, -offset) for offset in RING[1:]]

    cosine, sine = tables(lax.dynamic_slice_in_dim(block_order[0], me * 2, 2), head)

    def swap(v):
        return lax.ppermute(v, "ctx", other)

    other_tokens = swap(tokens)
    kv_mine, kv_theirs = call(
        project_kernel, [shape((rows, 2 * head), F32)] * 2, [SMEM] + [VMEM] * 3,
        (place, tokens, other_tokens, small_weights), 4 * rows * features * head)
    (projected,) = call(
        rotate_kernel, [shape((chips, rows, 2 * head))], [VMEM] * 4, (kv_mine, swap(kv_theirs), cosine, sine), 0)
    sources = (place, tokens, upstream, other_tokens, swap(upstream))
    halves = [shape((rows, 2 * width), F32)] * 2
    mine, theirs = call(
        first_partial_kernel, halves, [SMEM] + [VMEM] * 7,
        sources + tuple(held[:3]), 3 * rows * features * width)
    mine, theirs = call(
        last_partial_kernel, halves, [SMEM] + [VMEM] * 7,
        sources + (held[3], mine, theirs), rows * features * width,
        scratch=[pltpu.VMEM((rows, 2 * width), F32), pltpu.SemaphoreType.DMA], out_specs=[VMEM, HBM])
    own_part = to_chips(projected).reshape(seq // 2, 2 * head)
    own_part, theirs = lax.optimization_barrier((own_part, theirs))
    received = swap(theirs)
    other_part = swap(own_part)
    window = LONGEST + BLOCK
    grad_query, kept, sent = call(
        attention_kernel,
        [shape((rows, width)), shape((seq // 2, 2 * head)), shape((seq // 2, 2 * head))],
        [SMEM] * 3 + [VMEM] + [HBM] * 3 + [VMEM] * 2,
        (place, block_order, doc_lengths, mine, received, own_part, other_part, cosine, sine),
        20 * rows * heads * window * head,
        scratch=[pltpu.VMEM((rows, width), BF16), pltpu.VMEM((rows, width), BF16),
                 pltpu.VMEM((window, head), BF16), pltpu.VMEM((window, head), BF16),
                 pltpu.VMEM((seq, 2 * head), F32), pltpu.SMEM((seq // BLOCK,), jnp.int32),
                 pltpu.VMEM((rows, 2 * width), F32),
                 pltpu.VMEM((seq // 2, 2 * head), BF16), pltpu.VMEM((seq // 2, 2 * head), BF16),
                 pltpu.SemaphoreType.DMA((4,))],
        limit=28)
    pairs = (kept.astype(F32) + swap(sent).astype(F32)).astype(BF16)
    pieces, other_grad_query = lax.optimization_barrier(
        (to_chips(pairs).reshape(chips, rows, 2 * head), swap(grad_query)))
    (grads,) = call(owner_kernel, [shape((rows, 2 * head))], [VMEM] * 3, (pieces, cosine, sine), 0)
    other_grads = swap(grads)
    (parts,) = call(
        weight_kernel, [shape((chips, rows, head))], [SMEM] + [VMEM] * 4,
        (place, tokens, other_tokens, grads, other_grads), 2 * rows * features * head)
    input_mine, input_theirs = call(
        input_kernel, [shape((rows, features // 2))] * 2, [SMEM] + [VMEM] * 9,
        (place, grad_query, other_grad_query, grads, other_grads, small_weights, *held),
        2 * rows * features * (width + 2 * head))
    gathered, input_theirs = lax.optimization_barrier((to_chips(parts), input_theirs))
    grad_weight = jnp.sum(gathered.reshape(chips, rows, head).astype(F32), axis=0)
    group = dp
    while group > 4 and group % 2 == 0:
        group //= 2
    near = [[first + i for i in range(group)] for first in range(0, dp, group)]
    spread = jnp.broadcast_to(grad_weight.astype(BF16)[None], (group, rows, head))
    gathered = lax.all_to_all(spread, "dp", 0, 0, tiled=True, axis_index_groups=near)
    (grad_input,) = call(
        merge_kernel, [shape((rows, features))], [SMEM] + [VMEM] * 2,
        (place, input_mine, swap(input_theirs)), 0)
    grad_weight = jnp.sum(gathered.reshape(group, rows, head).astype(F32), axis=0)
    step = group
    while step < dp:
        received = lax.ppermute(grad_weight.astype(BF16), "dp", [(i, i ^ step) for i in range(dp)])
        received, grad_input = lax.optimization_barrier((received, grad_input))
        grad_weight = grad_weight.astype(BF16).astype(F32) + received.astype(F32)
        step *= 2
    return grad_input[None], grad_weight


def solution(mesh):
    placed = (
        P("dp", "ctx", None),
        P("dp", "ctx", None),
        P("ctx", None),
        P("ctx", None),
        P("ctx", None),
        P(None, "ctx"),
        P("dp", None),
        P("dp", None),
    )
    return jax.shard_map(
        on_device,
        mesh=mesh,
        in_specs=placed,
        out_specs=(P("dp", "ctx", None), P("ctx", None)),
        check_vma=False,
    )
```
